512 devices in a mesh: layer: 16 (over x_hi, y, core), plane: 32 (over x_lo, z).
Axes of the slice: x: 4 (x_hi: 2, x_lo: 2; x = x_hi * 2 + x_lo), y: 4, z: 16, core: 2. Of those that a mesh axis runs over, the one named last changes fastest.
Arguments:
- polar: float32 [16, 512, 512], P('layer', 'plane'), may hold values from 0.1 to 1.6
- azimuth: float32 [16, 512, 512], P('layer', 'plane'), may hold values from -3 to 3
- saturation: float32 [16, 512, 512], P('layer', 'plane'), may hold values from 0.5 to 1.5
- anisotropy: float32 [16, 512, 512], P('layer', 'plane'), may hold values from 0.3 to 1.5
- stiffness: float32 [16], P('layer'), may hold values from 0.35 to 0.7
- coupling: float32 [15], replicated, may hold values from -1 to 1
Outputs:
- field: float32 [16, 3, 512, 512], P('layer', None, 'plane')
- moment: float32 [16, 3, 512, 512], P('layer', None, 'plane')
The draws below stay inside these ranges and needn't reach their ends.
All inputs are finite; a program needn't handle non-finite values.
Results may differ from the reference program's by a relative error of at most 0.00005.
Values sent between devices are 32-bit elements; how exact they have to be, the bound alone decides.
A program may use at most 64 MiB of HBM per device.

```python
import math
import jax
import jax.numpy as jnp
from jax import lax

CELLS = 512
LAYERS = 16


def smooth_waves(key):
    first_key, second_key, phase_key = jax.random.split(key, 3)
    along_x = jax.random.randint(first_key, (LAYERS, 2), 1, 5)
    along_y = jax.random.randint(second_key, (LAYERS, 2), -4, 5)
    offset = jax.random.uniform(phase_key, (LAYERS, 2), jnp.float32, 0.0, 2.0 * jnp.pi)
    place = jnp.arange(CELLS, dtype=jnp.int32)
    turns = (along_x[:, :, None, None] * place[None, None, :, None] + along_y[:, :, None, None] * place[None, None, None, :]) % CELLS
    angle = turns.astype(jnp.float32) * (2.0 * jnp.pi / CELLS) + offset[:, :, None, None]
    waves = jnp.cos(angle)
    return 0.7 * waves[:, 0] + 0.3 * waves[:, 1]


def shared_wave(key):
    cycles = 183 * CELLS // 512
    place = jnp.arange(CELLS, dtype=jnp.int32)
    turns = cycles * place % CELLS
    offset = jax.random.uniform(key, (), jnp.float32, 0.0, 2.0 * jnp.pi)
    angle = turns.astype(jnp.float32) * (2.0 * jnp.pi / CELLS) + offset
    return jnp.cos(angle)[None, :, None]


def draw_polar(key, part):
    smooth = smooth_waves(jax.random.fold_in(key, 11))
    rough = jax.random.uniform(jax.random.fold_in(key, 12), (LAYERS, CELLS, CELLS), jnp.float32, -1.0, 1.0)
    common = shared_wave(jax.random.fold_in(key, 13))
    return 0.85 + 0.5 * common + 0.15 * smooth + 0.1 * rough


def draw_azimuth(key, part):
    smooth = smooth_waves(jax.random.fold_in(key, 21))
    rough = jax.random.uniform(jax.random.fold_in(key, 22), (LAYERS, CELLS, CELLS), jnp.float32, -1.0, 1.0)
    return 2.2 * smooth + 0.8 * rough


def steps_of(own_key, extent, cuts, low, largest):
    loudness = 1.0
    for dim, parts in cuts:
        heights = jax.random.uniform(jax.random.fold_in(jax.random.fold_in(own_key, 6), dim), (parts,), jnp.float32, low / len(cuts), largest / len(cuts))
        loudness = loudness * jnp.repeat(jnp.exp(heights), extent[dim] // parts).reshape((-1,) + (1,) * (len(extent) - 1 - dim))
    return loudness


def setup_inputs(seed: int = 0) -> dict:
    key_of = jax.random.split(jax.random.key(seed), 7)
    return {
        "polar": draw_polar(jax.random.fold_in(key_of[6], 71), 0),
        "azimuth": draw_azimuth(jax.random.fold_in(key_of[6], 71), 0),
        "saturation": jnp.clip(jnp.exp(math.log(1.5) - 1.0986123 * jax.random.uniform(key_of[2], (LAYERS, CELLS, CELLS), jnp.float32) ** steps_of(key_of[2], (LAYERS, CELLS, CELLS), ((0, 16), (1, 32)), -0.2, 0.2)), 0.5, 1.5),
        "anisotropy": jnp.clip(jnp.exp(math.log(1.5) - 1.60943787 * jax.random.uniform(key_of[3], (LAYERS, CELLS, CELLS), jnp.float32) ** steps_of(key_of[3], (LAYERS, CELLS, CELLS), ((0, 16), (1, 32)), -0.2, 0.2)), 0.3, 1.5),
        "stiffness": jnp.clip(jnp.exp(math.log(0.7) - 0.6931472 * jax.random.uniform(key_of[4], (LAYERS,), jnp.float32) ** steps_of(key_of[4], (LAYERS,), ((0, 16),), -0.2, 0.2)), 0.35, 0.7),
        "coupling": jnp.clip(jax.random.uniform(key_of[5], (LAYERS - 1,), jnp.float32, -1.0, 1.0), -1.0, 1.0),
    }


side_length = 512.0
spacing = 1.2
damping = 0.1
time_step = 0.1

def reference(polar, azimuth, saturation, anisotropy, stiffness, coupling):
    unit_moment = jnp.stack([jnp.sin(polar) * jnp.cos(azimuth), jnp.sin(polar) * jnp.sin(azimuth), jnp.cos(polar)], 1)
    magnet = unit_moment * saturation[:, None]
    pad_length = 2 * CELLS
    spectrum = jnp.fft.fft2(magnet, s=(pad_length, pad_length))
    wave_index = jnp.arange(pad_length, dtype=jnp.int32)
    folded = jnp.where(wave_index < CELLS, wave_index, wave_index - pad_length)
    wavenumber = jnp.pi * folded.astype(jnp.float32) / side_length
    wave_x = wavenumber[:, None]
    wave_y = wavenumber[None, :]
    magnitude = jnp.sqrt(wave_x * wave_x + wave_y * wave_y)
    nonzero = magnitude > 0.0
    safe = jnp.where(nonzero, magnitude, 1.0)
    unit_x = jnp.where(nonzero, wave_x / safe, 0.0)
    unit_y = jnp.where(nonzero, wave_y / safe, 0.0)
    self_part = jnp.where(nonzero, -jnp.expm1(-safe) / safe, 1.0)
    half_sinh = jnp.sinh(0.5 * safe)
    mutual = jnp.where(nonzero, 2.0 * half_sinh * half_sinh / safe, 0.0)
    decay = jnp.exp(-spacing * magnitude)
    inplane = unit_x * spectrum[:, 0] + unit_y * spectrum[:, 1]
    upward = spectrum[:, 2] - 1j * inplane
    downward = -spectrum[:, 2] - 1j * inplane
    carry = jnp.zeros_like(upward[0])
    below_list = []
    for layer_number in range(LAYERS):
        below_list.append(carry)
        carry = decay * (carry + upward[layer_number])
    carry = jnp.zeros_like(upward[0])
    above_list = [None] * LAYERS
    for layer_number in range(LAYERS - 1, -1, -1):
        above_list[layer_number] = carry
        carry = decay * (carry + downward[layer_number])
    below = jnp.stack(below_list)
    above = jnp.stack(above_list)
    total = below + above
    differ = below - above
    field_x = -(1.0 - self_part) * unit_x * inplane - 1j * unit_x * mutual * total
    field_y = -(1.0 - self_part) * unit_y * inplane - 1j * unit_y * mutual * total
    field_z = -self_part * spectrum[:, 2] + mutual * differ
    demag = jnp.real(jnp.fft.ifft2(jnp.stack([field_x, field_y, field_z], 1))[..., :CELLS, :CELLS])
    padded = jnp.pad(unit_moment, ((1, 1), (0, 0), (1, 1), (1, 1)))
    beside = padded[1:-1, :, :-2, 1:-1] + padded[1:-1, :, 2:, 1:-1]
    beside = beside + padded[1:-1, :, 1:-1, :-2] + padded[1:-1, :, 1:-1, 2:]
    nothing = jnp.zeros((1,), coupling.dtype)
    lower_link = jnp.concatenate([nothing, coupling])
    upper_link = jnp.concatenate([coupling, nothing])
    exchange = stiffness[:, None, None, None] * beside
    exchange = exchange + lower_link[:, None, None, None] * padded[:-2, :, 1:-1, 1:-1]
    exchange = exchange + upper_link[:, None, None, None] * padded[2:, :, 1:-1, 1:-1]
    zeros_plane = jnp.zeros_like(anisotropy)
    uniaxial = jnp.stack([zeros_plane, zeros_plane, anisotropy * unit_moment[:, 2]], 1)
    field = demag + exchange + uniaxial
    first_cross = jnp.cross(unit_moment, field, axis=1)
    second_cross = jnp.cross(unit_moment, first_cross, axis=1)
    torque = -(first_cross + damping * second_cross) / (1.0 + damping * damping)
    stepped = unit_moment + time_step * torque
    length = jnp.sqrt(lax.optimization_barrier(jnp.sum(stepped * stepped, axis=1, keepdims=True)))
    return (field, stepped / length)
```

```python
import functools
import math

import jax
import jax.numpy as jnp
import ml_dtypes
import numpy as np
from jax import lax
from jax.experimental import pallas as pl
from jax.experimental.pallas import tpu as pltpu
from jax.sharding import PartitionSpec as P

side_length = 512.0
spacing = 1.2
damping = 0.1
time_step = 0.1

CELLS = 512
PAD = 2 * CELLS
LAYERS = 16
RING = 16
SLAB = 32
MESH = pl.DeviceIdType.MESH
f32 = jnp.float32
bf16 = jnp.bfloat16


def halves(table):
    high = table.astype(ml_dtypes.bfloat16)
    low = (table - high.astype(np.float64)).astype(ml_dtypes.bfloat16)
    return high, low


@functools.lru_cache(None)
def transforms():
    column = np.arange(PAD)
    pair, part = column // 128, column // 64 % 2
    wave = (2 * pair + column % 2) * SLAB + column // 2 % SLAB
    place = np.arange(CELLS)
    angle = (place[:, None] * wave[None, :] % PAD) * (2.0 * np.pi / PAD)
    along_y = np.where(part[None, :] == 0, np.cos(angle), np.sin(angle))
    alternating = np.where(place % 2 == 0, 1.0, -1.0)
    along_y[:, (wave == 0) & (part == 1)] = alternating[:, None]
    row = np.arange(CELLS)
    x = row // 256 * 256 + row // 8 % 16 * 16 + row // 128 % 2 * 8 + row % 8
    angle = (x[:, None] * np.arange(CELLS)[None, :] % PAD) * (2.0 * np.pi / PAD)
    sine = np.sin(angle)
    sine[:, 0] = np.where(x % 2 == 0, 1.0, -1.0)
    along_x = np.concatenate([np.cos(angle), sine], 1)
    return halves(along_y) + halves(along_x)


def polynomial(x, coefficients):
    total = jnp.full_like(x, coefficients[-1])
    for c in coefficients[-2::-1]:
        total = total * x + c
    return total


SIN = [(-1.0) ** n / math.factorial(2 * n + 1) for n in range(7)]
COS = [(-1.0) ** n / math.factorial(2 * n) for n in range(8)]
SINH = [1.0 / math.factorial(2 * n + 1) for n in range(11)]


def sin_cos(x):
    square = x * x
    return x * polynomial(square, SIN), polynomial(square, COS)


def unit_moment(polar, azimuth):
    sin_p, cos_p = sin_cos(polar)
    s, c = sin_cos(0.5 * azimuth)
    return sin_p * (1.0 - 2.0 * s * s), sin_p * (2.0 * s * c), cos_p


def product(left, high_ref, low_ref, transposed):
    high = left.astype(bf16)
    low = (left - high.astype(f32)).astype(bf16)
    rows = left.shape[0]
    dims = (((1,), (1 if transposed else 0,)), ((), ()))
    both = lax.dot_general(
        jnp.concatenate([high, low], 0), high_ref[...], dims, preferred_element_type=f32
    )
    rest = lax.dot_general(high, low_ref[...], dims, preferred_element_type=f32)
    return both[:rows] + both[rows:] + rest


def even_lanes():
    return lax.broadcasted_iota(jnp.int32, (8, 128), 1) % 2 == 0


def forward_y(m, saturation, wyh, wyl, s1):
    rows = [m[c][8 * h : 8 * h + 8] * saturation[8 * h : 8 * h + 8] for h in range(2) for c in range(3)]
    y = product(jnp.concatenate(rows, 0), wyh, wyl, False)
    even = even_lanes()
    for c in range(3):
        for p in range(8):
            upper = y[8 * c : 8 * c + 8, 128 * p : 128 * p + 128]
            lower = y[24 + 8 * c : 32 + 8 * c, 128 * p : 128 * p + 128]
            s1[2 * p, c] = jnp.where(even, upper, pltpu.roll(lower, 1, 1))
            s1[2 * p + 1, c] = jnp.where(even, pltpu.roll(upper, 127, 1), lower)


def turn_in(r1, s2):
    for c in range(3):
        block = r1[:, c].reshape(128, 128).T
        for b in range(2):
            s2[pl.ds(2 * c + b, 64, stride=8), :] = block[64 * b : 64 * b + 64]


def spectral_tables(fy, tb):
    sub = lax.broadcasted_iota(jnp.int32, (8, 128), 0)
    fx = sub % 4 * 128 + lax.broadcasted_iota(jnp.int32, (8, 128), 1)
    second = sub // 4 == 1
    sign = jnp.where(second, 1.0, -1.0)
    edge_x = fx == 0
    edge_y = jnp.full((8, 128), fy) == 0
    for v in range(2):
        sine_y = second if v == 0 else jnp.logical_not(second)
        high_x = jnp.logical_and(edge_x, second)
        high_y = jnp.logical_and(edge_y, sine_y)
        wave_x = jnp.where(high_x, CELLS, fx).astype(f32) * (math.pi / side_length)
        wave_y = jnp.where(high_y, CELLS, fy).astype(f32) * (math.pi / side_length)
        k = jnp.sqrt(wave_x * wave_x + wave_y * wave_y)
        nonzero = k > 0.0
        safe = jnp.where(nonzero, k, 1.0)
        inverse = 1.0 / safe
        half = 0.5 * safe
        ratio = polynomial(half * half, SINH)
        self_part = jnp.where(nonzero, jnp.exp(-half) * ratio, 1.0)
        mutual = jnp.where(nonzero, half * ratio * ratio, 0.0)
        weight = jnp.where(edge_x, 1.0, 2.0) * jnp.where(edge_y, 1.0, 2.0) * (1.0 / (PAD * PAD))
        ux, uy = wave_x * inverse, wave_y * inverse
        tb[v, 0] = jnp.exp(-spacing * k)
        tb[v, 1] = weight * (1.0 - self_part)
        tb[v, 2] = weight * mutual
        tb[v, 3] = weight * self_part
        tb[v, 4] = jnp.where(edge_x, 0.0, sign * ux)
        tb[v, 5] = jnp.where(edge_y, 0.0, sign * uy)
        tb[v, 6] = jnp.where(high_x, ux, 0.0)
        tb[v, 7] = jnp.where(high_y, uy, 0.0)


ORDER = [(0, 0), (1, 1), (0, 1), (1, 0)]
ORDER_X = [(1, 1), (0, 0), (1, 0), (0, 1)]


def tile_row(c, tg, cls, lb):
    return ((c * 2 + tg) * 16 + cls * 4 + lb) * 8


def transform_x(r2, wxh, wxl, zs):
    columns = []
    for x_lo in range(2):
        for h in range(2):
            parts = [r2[pl.ds(x_lo * 16 + h * 8 + q, 16, stride=32), :] for q in range(6)]
            columns.append(jnp.concatenate(parts, 0))
    z = product(jnp.concatenate(columns, 1), wxh, wxl, False)
    for c in range(3):
        for cls, (a, b) in enumerate(ORDER_X if c == 0 else ORDER):
            for tg in range(2):
                for lb in range(4):
                    row = (2 * c + b) * 16 + tg * 8
                    lane = a * 512 + lb * 128
                    zs[pl.ds(tile_row(c, tg, cls, lb), 8), :] = z[row : row + 8, lane : lane + 128]


def couple(zs, tb, ws):
    def at(c, t, v):
        return pl.ds(tile_row(c, t // 8, 2 * v, 0) + t % 8, 8, stride=8)

    for v in range(2):
        other = 1 - v
        decay, direct, mutual = tb[v, 0], tb[v, 1], tb[v, 2]
        ux, uy, lone_x, lone_y = tb[v, 4], tb[v, 5], tb[v, 6], tb[v, 7]
        if v == 1:
            uy = -uy
        carry = jnp.zeros((8, 128), f32)
        carry_lone = jnp.zeros((8, 128), f32)
        for t in range(LAYERS):
            r = ux * zs[at(0, t, other), :] + uy * zs[at(1, t, other), :]
            lone = lone_x * pltpu.roll(zs[at(0, t, v), :], 4, 0) + lone_y * zs[at(1, t, v), :]
            ws[v, t, 0] = r
            ws[v, t, 1] = lone
            ws[v, t, 2] = carry
            ws[v, t, 3] = carry_lone
            carry = decay * (carry + (zs[at(2, t, v), :] + r))
            carry_lone = decay * (carry_lone + lone)
    for v in range(2):
        decay, direct, mutual = tb[v, 0], tb[v, 1], tb[v, 2]
        carry = jnp.zeros((8, 128), f32)
        carry_lone = jnp.zeros((8, 128), f32)
        for t in range(LAYERS - 1, -1, -1):
            r, lone = ws[v, t, 0], ws[v, t, 1]
            below, below_lone = ws[v, t, 2], ws[v, t, 3]
            z = zs[at(2, t, v), :]
            ws[v, t, 0] = direct * r + mutual * (below + carry)
            ws[v, t, 1] = direct * lone + mutual * (below_lone + carry_lone)
            zs[at(2, t, v), :] = mutual * (below - carry) - tb[v, 3] * z
            carry = decay * (carry + (r - z))
            carry_lone = decay * (carry_lone + lone)
    for v in range(2):
        other = 1 - v
        ux, uy, lone_x, lone_y = tb[other, 4], tb[v, 5], tb[v, 6], tb[v, 7]
        if v == 1:
            uy = -uy
        for t in range(LAYERS):
            h, lone = ws[other, t, 0], ws[v, t, 1]
            zs[at(0, t, v), :] = -ux * h - pltpu.roll(lone_x * lone, 4, 0)
            zs[at(1, t, v), :] = uy * h - lone_y * lone


def return_x(zs, wxh, wxl, s3):
    rows = []
    for c in range(3):
        order = ORDER_X if c == 0 else ORDER
        for b in range(2):
            for tg in range(2):
                lanes = [
                    zs[pl.ds(tile_row(c, tg, order.index((a, b)), lb), 8), :] for a in range(2) for lb in range(4)
                ]
                rows.append(jnp.concatenate(lanes, 1))
    out = product(jnp.concatenate(rows, 0), wxh, wxl, True)
    for x_lo in range(2):
        for h in range(2):
            lane = (x_lo * 2 + h) * 128
            for q in range(6):
                s3[pl.ds(x_lo * 16 + h * 8 + q, 16, stride=32), :] = out[16 * q : 16 * q + 16, lane : lane + 128]


def turn_out(r3, s4):
    for c in range(3):
        parts = [r3[pl.ds(2 * c + b, 64, stride=8), :] for b in range(2)]
        s4[:, c] = jnp.concatenate(parts, 0).T.reshape(16, 8, 128)


def inverse_y(r4, wyh, wyl):
    even = even_lanes()
    upper, lower = [], []
    for c in range(3):
        up, low = [], []
        for p in range(8):
            first, second = r4[2 * p, c], r4[2 * p + 1, c]
            up.append(jnp.where(even, first, pltpu.roll(second, 1, 1)))
            low.append(jnp.where(even, pltpu.roll(first, 127, 1), second))
        upper.append(jnp.concatenate(up, 1))
        lower.append(jnp.concatenate(low, 1))
    out = product(jnp.concatenate(upper + lower, 0), wyh, wyl, True)
    return [jnp.concatenate([out[8 * c : 8 * c + 8], out[24 + 8 * c : 32 + 8 * c]], 0) for c in range(3)]


def cross_product(a, b):
    return (a[1] * b[2] - a[2] * b[1], a[2] * b[0] - a[0] * b[2], a[0] * b[1] - a[1] * b[0])


def other_fields(m, first_row, last_row, lower_m, upper_m, stiffness, lower_link, upper_link, anisotropy):
    lane = lax.broadcasted_iota(jnp.int32, (16, 512), 1)
    fields = []
    for c in range(3):
        beside = jnp.concatenate([first_row[c], m[c][:15]], 0) + jnp.concatenate([m[c][1:], last_row[c]], 0)
        beside = beside + jnp.where(lane == 0, 0.0, pltpu.roll(m[c], 1, 1))
        beside = beside + jnp.where(lane == 511, 0.0, pltpu.roll(m[c], 511, 1))
        fields.append(stiffness * beside + lower_link * lower_m[c] + upper_link * upper_m[c])
    fields[2] = fields[2] + anisotropy * m[2]
    return fields


def step(m, field):
    first = cross_product(m, field)
    second = cross_product(m, first)
    scale = -time_step / (1.0 + damping * damping)
    stepped = [m[c] + scale * (first[c] + damping * second[c]) for c in range(3)]
    inverse = lax.rsqrt(stepped[0] * stepped[0] + stepped[1] * stepped[1] + stepped[2] * stepped[2])
    return [s * inverse for s in stepped]


def kernel(
    polar, azimuth, saturation, anisotropy, stiffness, coupling, wyh_any, wyl_any, wxh_any, wxl_any,
    field_out, moment_out,
    wyh, wyl, wxh, wxl, s1, r1, s2, r2, s3, r3, s4, r4, zs, ws, tb, near, edge_out, edge_in, rest,
    load_sem, send_sem, recv_sem, near_send, near_recv, edge_send, edge_recv,
):
    t = lax.axis_index("layer")
    p = lax.axis_index("plane")
    z = lax.rem(p, RING)
    x_lo = lax.div(p, RING)
    f = t * 2 + x_lo

    loads = [
        pltpu.make_async_copy(src, dst, load_sem.at[i])
        for i, (src, dst) in enumerate([(wyh_any, wyh), (wyl_any, wyl), (wxh_any, wxh), (wxl_any, wxl)])
    ]
    for load in loads:
        load.start()

    def ring_device(i):
        dist = RING // 2 - lax.div(i + 1, 2)
        there = lax.rem(z + jnp.where(lax.rem(i, 2) == 1, dist, RING - dist), RING)
        return there, (t, x_lo * RING + there)

    def slab_device(i):
        there = lax.rem(f + 1 + i, SLAB)
        return there, (lax.div(there, 2), lax.rem(there, 2) * RING + z)

    next_plane = (t, lax.rem(p + 1, 2 * RING))
    last_plane = (t, lax.rem(p + 2 * RING - 1, 2 * RING))
    next_layer = (lax.rem(t + 1, LAYERS), p)
    last_layer = (lax.rem(t + LAYERS - 1, LAYERS), p)

    barrier = pltpu.get_barrier_semaphore()

    def greet(where):
        def one(i, carry):
            pl.semaphore_signal(barrier, inc=1, device_id=where(i)[1], device_id_type=MESH)
            return carry

        return one

    lax.fori_loop(0, RING - 1, greet(ring_device), 0)
    lax.fori_loop(0, SLAB - 1, greet(slab_device), 0)
    for there in (next_plane, last_plane):
        pl.semaphore_signal(barrier, inc=1, device_id=there, device_id_type=MESH)

    m = unit_moment(polar[0], azimuth[0])
    edge_out[...] = jnp.zeros((2, 16, 128), f32)
    for side, row in enumerate((0, 15)):
        for c in range(3):
            for lb in range(4):
                edge_out[side, c * 4 + lb : c * 4 + lb + 1, :] = m[c][row : row + 1, 128 * lb : 128 * lb + 128]
    s2[...] = jnp.zeros((512, 128), f32)
    s3[...] = jnp.zeros((512, 128), f32)
    loads[0].wait()
    loads[1].wait()
    forward_y(m, saturation[0], wyh, wyl, s1)

    pl.semaphore_wait(barrier, RING - 1 + SLAB - 1 + 2)

    def remote(src, dst, sem, there):
        return pltpu.make_async_remote_copy(
            src_ref=src, dst_ref=dst, send_sem=sem[0], recv_sem=sem[1], device_id=there, device_id_type=MESH
        )

    def ring_send(src, dst, n):
        def one(i, carry):
            there, device = ring_device(i)
            remote(src.at[there], dst.at[z], (send_sem.at[n], recv_sem.at[n]), device).start()
            return carry

        lax.fori_loop(0, RING - 1, one, 0)
        pltpu.make_async_copy(src.at[z], dst.at[z], recv_sem.at[n]).start()

    def rows_of(ref, i):
        return ref.at[pl.ds(pl.multiple_of(i * 16, 16), 16)]

    def slab_send(src, dst, n):
        def one(i, carry):
            there, device = slab_device(i)
            remote(rows_of(src, there), rows_of(dst, f), (send_sem.at[n], recv_sem.at[n]), device).start()
            return carry

        lax.fori_loop(0, SLAB - 1, one, 0)
        pltpu.make_async_copy(rows_of(src, f), rows_of(dst, f), recv_sem.at[n]).start()

    def received(dst, n):
        pltpu.make_async_copy(dst, dst, recv_sem.at[n]).wait()

    ring_send(s1, r1, 0)
    sides = []
    for i, (ref, side, there) in enumerate(
        [(polar, 0, next_layer), (azimuth, 0, next_layer), (polar, 1, last_layer), (azimuth, 1, last_layer)]
    ):
        sides.append(remote(ref.at[0], near.at[side, i % 2], (near_send.at[i], near_recv.at[i]), there))
    for side, there in ((0, last_plane), (1, next_plane)):
        sides.append(
            remote(edge_out.at[side], edge_in.at[1 - side], (edge_send.at[side], edge_recv.at[side]), there)
        )
    for copy in sides:
        copy.start()

    spectral_tables(z * SLAB + f, tb)
    for copy in sides:
        copy.wait_recv()
    lower_m = unit_moment(near[0, 0], near[0, 1])
    upper_m = unit_moment(near[1, 0], near[1, 1])
    lower_link = jnp.where(t > 0, coupling[jnp.maximum(t - 1, 0)], 0.0)
    upper_link = jnp.where(t < LAYERS - 1, coupling[jnp.minimum(t, LAYERS - 2)], 0.0)

    def edge_row(side, present):
        rows = []
        for c in range(3):
            lanes = [edge_in[side, c * 4 + lb : c * 4 + lb + 1, :] for lb in range(4)]
            rows.append(jnp.where(present, jnp.concatenate(lanes, 1), 0.0))
        return rows

    m = unit_moment(polar[0], azimuth[0])
    fields = other_fields(
        m, edge_row(0, p > 0), edge_row(1, p < 2 * RING - 1), lower_m, upper_m,
        stiffness[0], lower_link, upper_link, anisotropy[0],
    )
    for c in range(3):
        rest[c] = fields[c]
        rest[3 + c] = m[c]

    received(r1, 0)
    turn_in(r1, s2)
    slab_send(s2, r2, 1)
    loads[2].wait()
    loads[3].wait()
    received(r2, 1)
    transform_x(r2, wxh, wxl, zs)
    couple(zs, tb, ws)
    return_x(zs, wxh, wxl, s3)
    slab_send(s3, r3, 2)
    received(r3, 2)
    turn_out(r3, s4)
    ring_send(s4, r4, 3)
    received(r4, 3)
    demag = inverse_y(r4, wyh, wyl)
    m = [rest[3 + c] for c in range(3)]
    field = [demag[c] + rest[c] for c in range(3)]
    moment = step(m, field)
    for c in range(3):
        field_out[0, c] = field[c]
        moment_out[0, c] = moment[c]

    for copy in sides:
        copy.wait_send()
    ring_part = s1.at[pl.ds(0, RING - 1)]
    slab_part = s2.at[pl.ds(0, 16 * (SLAB - 1))]
    for n, part in ((0, ring_part), (1, slab_part), (2, slab_part), (3, ring_part)):
        pltpu.make_async_copy(part, part, send_sem.at[n]).wait()


def body(polar, azimuth, saturation, anisotropy, stiffness, coupling):
    vmem = pl.BlockSpec(memory_space=pltpu.VMEM)
    smem = pl.BlockSpec(memory_space=pltpu.SMEM)
    hbm = pl.BlockSpec(memory_space=pl.ANY)
    out = jax.ShapeDtypeStruct((1, 3, 16, CELLS), f32)
    dma = pltpu.SemaphoreType.DMA
    ring = pltpu.VMEM((RING, 3, 8, 128), f32)
    slab = pltpu.VMEM((SLAB * 16, 128), f32)
    return pl.pallas_call(
        kernel,
        out_shape=(out, out),
        in_specs=[vmem] * 4 + [smem] * 2 + [hbm] * 4,
        out_specs=(vmem, vmem),
        scratch_shapes=[
            pltpu.VMEM((CELLS, PAD), bf16),
            pltpu.VMEM((CELLS, PAD), bf16),
            pltpu.VMEM((CELLS, PAD), bf16),
            pltpu.VMEM((CELLS, PAD), bf16),
            ring, ring, slab, slab, slab, slab, ring, ring,
            pltpu.VMEM((3 * 2 * 16 * 8, 128), f32),
            pltpu.VMEM((2, LAYERS, 4, 8, 128), f32),
            pltpu.VMEM((2, 8, 8, 128), f32),
            pltpu.VMEM((2, 2, 16, CELLS), f32),
            pltpu.VMEM((2, 16, 128), f32),
            pltpu.VMEM((2, 16, 128), f32),
            pltpu.VMEM((6, 16, CELLS), f32),
            dma((4,)), dma((4,)), dma((4,)), dma((4,)), dma((4,)), dma((2,)), dma((2,)),
        ],
        compiler_params=pltpu.CompilerParams(
            collective_id=0, has_side_effects=True, vmem_limit_bytes=40 * 1024 * 1024
        ),
        cost_estimate=pl.CostEstimate(flops=10**9, bytes_accessed=5 * 10**6, transcendentals=0),
        name="fields",
    )(polar, azimuth, saturation, anisotropy, stiffness, coupling, *transforms())


def solution(mesh):
    placed = (
        P("layer", "plane", None),
        P("layer", "plane", None),
        P("layer", "plane", None),
        P("layer", "plane", None),
        P("layer"),
        P(),
    )
    return jax.shard_map(
        body,
        mesh=mesh,
        in_specs=placed,
        out_specs=(P("layer", None, "plane", None), P("layer", None, "plane", None)),
        check_vma=False,
    )
```

```python
import functools
import math

import jax
import jax.numpy as jnp
import ml_dtypes
import numpy as np
from jax import lax
from jax.experimental import pallas as pl
from jax.experimental.pallas import tpu as pltpu
from jax.sharding import PartitionSpec as P

side_length = 512.0
spacing = 1.2
damping = 0.1
time_step = 0.1

CELLS = 512
PAD = 2 * CELLS
LAYERS = 16
RING = 16
SLAB = 32
MESH = pl.DeviceIdType.MESH
f32 = jnp.float32
bf16 = jnp.bfloat16


def halves(table):
    high = table.astype(ml_dtypes.bfloat16)
    low = (table - high.astype(np.float64)).astype(ml_dtypes.bfloat16)
    return high, low


@functools.lru_cache(None)
def transforms():
    column = np.arange(PAD)
    pair, part = column // 128, column // 64 % 2
    wave = (2 * pair + column % 2) * SLAB + column // 2 % SLAB
    place = np.arange(CELLS)
    angle = (place[:, None] * wave[None, :] % PAD) * (2.0 * np.pi / PAD)
    along_y = np.where(part[None, :] == 0, np.cos(angle), np.sin(angle))
    alternating = np.where(place % 2 == 0, 1.0, -1.0)
    along_y[:, (wave == 0) & (part == 1)] = alternating[:, None]
    row = np.arange(CELLS)
    x = row // 256 * 256 + row // 8 % 16 * 16 + row // 128 % 2 * 8 + row % 8
    angle = (x[:, None] * np.arange(CELLS)[None, :] % PAD) * (2.0 * np.pi / PAD)
    sine = np.sin(angle)
    sine[:, 0] = np.where(x % 2 == 0, 1.0, -1.0)
    along_x = np.concatenate([np.cos(angle), sine], 1)
    return halves(along_y) + halves(along_x)


def polynomial(x, coefficients):
    total = jnp.full_like(x, coefficients[-1])
    for c in coefficients[-2::-1]:
        total = total * x + c
    return total


SIN = [(-1.0) ** n / math.factorial(2 * n + 1) for n in range(7)]
COS = [(-1.0) ** n / math.factorial(2 * n) for n in range(8)]
SINH = [1.0 / math.factorial(2 * n + 1) for n in range(11)]


def sin_cos(x):
    square = x * x
    return x * polynomial(square, SIN), polynomial(square, COS)


def unit_moment(polar, azimuth):
    sin_p, cos_p = sin_cos(polar)
    s, c = sin_cos(0.5 * azimuth)
    return sin_p * (1.0 - 2.0 * s * s), sin_p * (2.0 * s * c), cos_p


def product(left, high_ref, low_ref, transposed):
    high = left.astype(bf16)
    low = (left - high.astype(f32)).astype(bf16)
    rows = left.shape[0]
    dims = (((1,), (1 if transposed else 0,)), ((), ()))
    both = lax.dot_general(
        jnp.concatenate([high, low], 0), high_ref[...], dims, preferred_element_type=f32
    )
    rest = lax.dot_general(high, low_ref[...], dims, preferred_element_type=f32)
    return both[:rows] + both[rows:] + rest


def even_lanes():
    return lax.broadcasted_iota(jnp.int32, (8, 128), 1) % 2 == 0


def forward_y(m, saturation, wyh, wyl, s1):
    rows = [m[c][8 * h : 8 * h + 8] * saturation[8 * h : 8 * h + 8] for h in range(2) for c in range(3)]
    y = product(jnp.concatenate(rows, 0), wyh, wyl, False)
    even = even_lanes()
    for c in range(3):
        for p in range(8):
            upper = y[8 * c : 8 * c + 8, 128 * p : 128 * p + 128]
            lower = y[24 + 8 * c : 32 + 8 * c, 128 * p : 128 * p + 128]
            s1[2 * p, c] = jnp.where(even, upper, pltpu.roll(lower, 1, 1))
            s1[2 * p + 1, c] = jnp.where(even, pltpu.roll(upper, 127, 1), lower)


def turn_in(r1, s2):
    for c in range(3):
        block = r1[:, c].reshape(128, 128).T
        for b in range(2):
            s2[pl.ds(2 * c + b, 64, stride=8), :] = block[64 * b : 64 * b + 64]


def spectral_tables(fy, tb):
    sub = lax.broadcasted_iota(jnp.int32, (8, 128), 0)
    fx = sub % 4 * 128 + lax.broadcasted_iota(jnp.int32, (8, 128), 1)
    second = sub // 4 == 1
    sign = jnp.where(second, 1.0, -1.0)
    edge_x = fx == 0
    edge_y = jnp.full((8, 128), fy) == 0
    for v in range(2):
        sine_y = second if v == 0 else jnp.logical_not(second)
        high_x = jnp.logical_and(edge_x, second)
        high_y = jnp.logical_and(edge_y, sine_y)
        wave_x = jnp.where(high_x, CELLS, fx).astype(f32) * (math.pi / side_length)
        wave_y = jnp.where(high_y, CELLS, fy).astype(f32) * (math.pi / side_length)
        k = jnp.sqrt(wave_x * wave_x + wave_y * wave_y)
        nonzero = k > 0.0
        safe = jnp.where(nonzero, k, 1.0)
        inverse = 1.0 / safe
        half = 0.5 * safe
        ratio = polynomial(half * half, SINH)
        self_part = jnp.where(nonzero, jnp.exp(-half) * ratio, 1.0)
        mutual = jnp.where(nonzero, half * ratio * ratio, 0.0)
        weight = jnp.where(edge_x, 1.0, 2.0) * jnp.where(edge_y, 1.0, 2.0) * (1.0 / (PAD * PAD))
        ux, uy = wave_x * inverse, wave_y * inverse
        tb[v, 0] = jnp.exp(-spacing * k)
        tb[v, 1] = weight * (1.0 - self_part)
        tb[v, 2] = weight * mutual
        tb[v, 3] = weight * self_part
        tb[v, 4] = jnp.where(edge_x, 0.0, sign * ux)
        tb[v, 5] = jnp.where(edge_y, 0.0, sign * uy)
        tb[v, 6] = jnp.where(high_x, ux, 0.0)
        tb[v, 7] = jnp.where(high_y, uy, 0.0)


ORDER = [(0, 0), (1, 1), (0, 1), (1, 0)]
ORDER_X = [(1, 1), (0, 0), (1, 0), (0, 1)]


def tile_row(c, tg, cls, lb):
    return ((c * 2 + tg) * 16 + cls * 4 + lb) * 8


def transform_x(r2, wxh, wxl, zs):
    columns = []
    for x_lo in range(2):
        for h in range(2):
            parts = [r2[pl.ds(x_lo * 16 + h * 8 + q, 16, stride=32), :] for q in range(6)]
            columns.append(jnp.concatenate(parts, 0))
    z = product(jnp.concatenate(columns, 1), wxh, wxl, False)
    for c in range(3):
        for cls, (a, b) in enumerate(ORDER_X if c == 0 else ORDER):
            for tg in range(2):
                for lb in range(4):
                    row = (2 * c + b) * 16 + tg * 8
                    lane = a * 512 + lb * 128
                    zs[pl.ds(tile_row(c, tg, cls, lb), 8), :] = z[row : row + 8, lane : lane + 128]


def couple(zs, tb, ws):
    def at(c, t, v):
        return pl.ds(tile_row(c, t // 8, 2 * v, 0) + t % 8, 8, stride=8)

    for v in range(2):
        other = 1 - v
        decay, direct, mutual = tb[v, 0], tb[v, 1], tb[v, 2]
        ux, uy, lone_x, lone_y = tb[v, 4], tb[v, 5], tb[v, 6], tb[v, 7]
        if v == 1:
            uy = -uy
        carry = jnp.zeros((8, 128), f32)
        carry_lone = jnp.zeros((8, 128), f32)
        for t in range(LAYERS):
            r = ux * zs[at(0, t, other), :] + uy * zs[at(1, t, other), :]
            lone = lone_x * pltpu.roll(zs[at(0, t, v), :], 4, 0) + lone_y * zs[at(1, t, v), :]
            ws[v, t, 0] = r
            ws[v, t, 1] = lone
            ws[v, t, 2] = carry
            ws[v, t, 3] = carry_lone
            carry = decay * (carry + (zs[at(2, t, v), :] + r))
            carry_lone = decay * (carry_lone + lone)
    for v in range(2):
        decay, direct, mutual = tb[v, 0], tb[v, 1], tb[v, 2]
        carry = jnp.zeros((8, 128), f32)
        carry_lone = jnp.zeros((8, 128), f32)
        for t in range(LAYERS - 1, -1, -1):
            r, lone = ws[v, t, 0], ws[v, t, 1]
            below, below_lone = ws[v, t, 2], ws[v, t, 3]
            z = zs[at(2, t, v), :]
            ws[v, t, 0] = direct * r + mutual * (below + carry)
            ws[v, t, 1] = direct * lone + mutual * (below_lone + carry_lone)
            zs[at(2, t, v), :] = mutual * (below - carry) - tb[v, 3] * z
            carry = decay * (carry + (r - z))
            carry_lone = decay * (carry_lone + lone)
    for v in range(2):
        other = 1 - v
        ux, uy, lone_x, lone_y = tb[other, 4], tb[v, 5], tb[v, 6], tb[v, 7]
        if v == 1:
            uy = -uy
        for t in range(LAYERS):
            h, lone = ws[other, t, 0], ws[v, t, 1]
            zs[at(0, t, v), :] = -ux * h - pltpu.roll(lone_x * lone, 4, 0)
            zs[at(1, t, v), :] = uy * h - lone_y * lone


def return_x(zs, wxh, wxl, s3):
    rows = []
    for c in range(3):
        order = ORDER_X if c == 0 else ORDER
        for b in range(2):
            for tg in range(2):
                lanes = [
                    zs[pl.ds(tile_row(c, tg, order.index((a, b)), lb), 8), :] for a in range(2) for lb in range(4)
                ]
                rows.append(jnp.concatenate(lanes, 1))
    out = product(jnp.concatenate(rows, 0), wxh, wxl, True)
    for x_lo in range(2):
        for h in range(2):
            lane = (x_lo * 2 + h) * 128
            for q in range(6):
                s3[pl.ds(x_lo * 16 + h * 8 + q, 16, stride=32), :] = out[16 * q : 16 * q + 16, lane : lane + 128]


def turn_out(r3, s4):
    for c in range(3):
        parts = [r3[pl.ds(2 * c + b, 64, stride=8), :] for b in range(2)]
        s4[:, c] = jnp.concatenate(parts, 0).T.reshape(16, 8, 128)


def inverse_y(r4, wyh, wyl):
    even = even_lanes()
    upper, lower = [], []
    for c in range(3):
        up, low = [], []
        for p in range(8):
            first, second = r4[2 * p, c], r4[2 * p + 1, c]
            up.append(jnp.where(even, first, pltpu.roll(second, 1, 1)))
            low.append(jnp.where(even, pltpu.roll(first, 127, 1), second))
        upper.append(jnp.concatenate(up, 1))
        lower.append(jnp.concatenate(low, 1))
    out = product(jnp.concatenate(upper + lower, 0), wyh, wyl, True)
    return [jnp.concatenate([out[8 * c : 8 * c + 8], out[24 + 8 * c : 32 + 8 * c]], 0) for c in range(3)]


def cross_product(a, b):
    return (a[1] * b[2] - a[2] * b[1], a[2] * b[0] - a[0] * b[2], a[0] * b[1] - a[1] * b[0])


def other_fields(m, first_row, last_row, lower_m, upper_m, stiffness, lower_link, upper_link, anisotropy):
    lane = lax.broadcasted_iota(jnp.int32, (16, 512), 1)
    fields = []
    for c in range(3):
        beside = jnp.concatenate([first_row[c], m[c][:15]], 0) + jnp.concatenate([m[c][1:], last_row[c]], 0)
        beside = beside + jnp.where(lane == 0, 0.0, pltpu.roll(m[c], 1, 1))
        beside = beside + jnp.where(lane == 511, 0.0, pltpu.roll(m[c], 511, 1))
        fields.append(stiffness * beside + lower_link * lower_m[c] + upper_link * upper_m[c])
    fields[2] = fields[2] + anisotropy * m[2]
    return fields


def step(m, field):
    first = cross_product(m, field)
    second = cross_product(m, first)
    scale = -time_step / (1.0 + damping * damping)
    stepped = [m[c] + scale * (first[c] + damping * second[c]) for c in range(3)]
    inverse = lax.rsqrt(stepped[0] * stepped[0] + stepped[1] * stepped[1] + stepped[2] * stepped[2])
    return [s * inverse for s in stepped]


def kernel(
    polar_any, azimuth_any, saturation_any, anisotropy_any, stiffness_any, coupling_any,
    wyh_any, wyl_any, wxh_any, wxl_any,
    field_out, moment_out,
    polar, azimuth, saturation, anisotropy, stiffness, coupling,
    wyh, wyl, wxh, wxl, s1, r1, s2, r2, s3, r3, s4, r4, zs, ws, tb, near, edge_out, edge_in, rest,
    load_sem, send_sem, recv_sem, near_send, near_recv, edge_send, edge_recv,
):
    t = lax.axis_index("layer")
    p = lax.axis_index("plane")
    z = lax.rem(p, RING)
    x_lo = lax.div(p, RING)
    f = t * 2 + x_lo

    loads = [
        pltpu.make_async_copy(src, dst, load_sem.at[i])
        for i, (src, dst) in enumerate([
            (polar_any, polar), (azimuth_any, azimuth), (saturation_any, saturation), (wyh_any, wyh), (wyl_any, wyl),
            (anisotropy_any, anisotropy), (stiffness_any, stiffness), (coupling_any, coupling),
            (wxh_any, wxh), (wxl_any, wxl),
        ])
    ]
    for load in loads:
        load.start()

    def ring_device(i):
        dist = RING // 2 - lax.div(i + 1, 2)
        there = lax.rem(z + jnp.where(lax.rem(i, 2) == 1, dist, RING - dist), RING)
        return there, (t, x_lo * RING + there)

    def slab_device(i):
        there = lax.rem(f + 1 + i, SLAB)
        return there, (lax.div(there, 2), lax.rem(there, 2) * RING + z)

    next_plane = (t, lax.rem(p + 1, 2 * RING))
    last_plane = (t, lax.rem(p + 2 * RING - 1, 2 * RING))
    next_layer = (lax.rem(t + 1, LAYERS), p)
    last_layer = (lax.rem(t + LAYERS - 1, LAYERS), p)

    barrier = pltpu.get_barrier_semaphore()

    def greet(where):
        def one(i, carry):
            pl.semaphore_signal(barrier, inc=1, device_id=where(i)[1], device_id_type=MESH)
            return carry

        return one

    lax.fori_loop(0, RING - 1, greet(ring_device), 0)
    lax.fori_loop(0, SLAB - 1, greet(slab_device), 0)
    for there in (next_plane, last_plane):
        pl.semaphore_signal(barrier, inc=1, device_id=there, device_id_type=MESH)

    loads[0].wait()
    loads[1].wait()
    m = unit_moment(polar[0], azimuth[0])
    edge_out[...] = jnp.zeros((2, 16, 128), f32)
    for side, row in enumerate((0, 15)):
        for c in range(3):
            for lb in range(4):
                edge_out[side, c * 4 + lb : c * 4 + lb + 1, :] = m[c][row : row + 1, 128 * lb : 128 * lb + 128]
    s2[...] = jnp.zeros((512, 128), f32)
    s3[...] = jnp.zeros((512, 128), f32)
    for load in loads[2:5]:
        load.wait()
    forward_y(m, saturation[0], wyh, wyl, s1)

    pl.semaphore_wait(barrier, RING - 1 + SLAB - 1 + 2)

    def remote(src, dst, sem, there):
        return pltpu.make_async_remote_copy(
            src_ref=src, dst_ref=dst, send_sem=sem[0], recv_sem=sem[1], device_id=there, device_id_type=MESH
        )

    def ring_send(src, dst, n):
        def one(i, carry):
            there, device = ring_device(i)
            remote(src.at[there], dst.at[z], (send_sem.at[n], recv_sem.at[n]), device).start()
            return carry

        lax.fori_loop(0, RING - 1, one, 0)
        pltpu.make_async_copy(src.at[z], dst.at[z], recv_sem.at[n]).start()

    def rows_of(ref, i):
        return ref.at[pl.ds(pl.multiple_of(i * 16, 16), 16)]

    def slab_send(src, dst, n):
        def one(i, carry):
            there, device = slab_device(i)
            remote(rows_of(src, there), rows_of(dst, f), (send_sem.at[n], recv_sem.at[n]), device).start()
            return carry

        lax.fori_loop(0, SLAB - 1, one, 0)
        pltpu.make_async_copy(rows_of(src, f), rows_of(dst, f), recv_sem.at[n]).start()

    def received(dst, n):
        pltpu.make_async_copy(dst, dst, recv_sem.at[n]).wait()

    ring_send(s1, r1, 0)
    sides = []
    for i, (ref, side, there) in enumerate(
        [(polar, 0, next_layer), (azimuth, 0, next_layer), (polar, 1, last_layer), (azimuth, 1, last_layer)]
    ):
        sides.append(remote(ref.at[0], near.at[side, i % 2], (near_send.at[i], near_recv.at[i]), there))
    for side, there in ((0, last_plane), (1, next_plane)):
        sides.append(
            remote(edge_out.at[side], edge_in.at[1 - side], (edge_send.at[side], edge_recv.at[side]), there)
        )
    for copy in sides:
        copy.start()

    for load in loads[5:]:
        load.wait()
    spectral_tables(z * SLAB + f, tb)
    for copy in sides:
        copy.wait_recv()
    lower_m = unit_moment(near[0, 0], near[0, 1])
    upper_m = unit_moment(near[1, 0], near[1, 1])
    lower_link = jnp.where(t > 0, coupling[jnp.maximum(t - 1, 0)], 0.0)
    upper_link = jnp.where(t < LAYERS - 1, coupling[jnp.minimum(t, LAYERS - 2)], 0.0)

    def edge_row(side, present):
        rows = []
        for c in range(3):
            lanes = [edge_in[side, c * 4 + lb : c * 4 + lb + 1, :] for lb in range(4)]
            rows.append(jnp.where(present, jnp.concatenate(lanes, 1), 0.0))
        return rows

    m = unit_moment(polar[0], azimuth[0])
    fields = other_fields(
        m, edge_row(0, p > 0), edge_row(1, p < 2 * RING - 1), lower_m, upper_m,
        stiffness[0], lower_link, upper_link, anisotropy[0],
    )
    for c in range(3):
        rest[c] = fields[c]
        rest[3 + c] = m[c]

    received(r1, 0)
    turn_in(r1, s2)
    slab_send(s2, r2, 1)
    received(r2, 1)
    transform_x(r2, wxh, wxl, zs)
    couple(zs, tb, ws)
    return_x(zs, wxh, wxl, s3)
    slab_send(s3, r3, 2)
    received(r3, 2)
    turn_out(r3, s4)
    ring_send(s4, r4, 3)
    received(r4, 3)
    demag = inverse_y(r4, wyh, wyl)
    m = [rest[3 + c] for c in range(3)]
    field = [demag[c] + rest[c] for c in range(3)]
    moment = step(m, field)
    for c in range(3):
        field_out[0, c] = field[c]
        moment_out[0, c] = moment[c]

    for copy in sides:
        copy.wait_send()
    ring_part = s1.at[pl.ds(0, RING - 1)]
    slab_part = s2.at[pl.ds(0, 16 * (SLAB - 1))]
    for n, part in ((0, ring_part), (1, slab_part), (2, slab_part), (3, ring_part)):
        pltpu.make_async_copy(part, part, send_sem.at[n]).wait()


def body(polar, azimuth, saturation, anisotropy, stiffness, coupling):
    vmem = pl.BlockSpec(memory_space=pltpu.VMEM)
    hbm = pl.BlockSpec(memory_space=pltpu.HBM)
    out = jax.ShapeDtypeStruct((1, 3, 16, CELLS), f32)
    dma = pltpu.SemaphoreType.DMA
    ring = pltpu.VMEM((RING, 3, 8, 128), f32)
    slab = pltpu.VMEM((SLAB * 16, 128), f32)
    row_block = pltpu.VMEM((1, 16, CELLS), f32)
    return pl.pallas_call(
        kernel,
        out_shape=(out, out),
        in_specs=[hbm] * 10,
        out_specs=(vmem, vmem),
        scratch_shapes=[
            row_block, row_block, row_block, row_block,
            pltpu.SMEM((1,), f32), pltpu.SMEM((LAYERS - 1,), f32),
            pltpu.VMEM((CELLS, PAD), bf16),
            pltpu.VMEM((CELLS, PAD), bf16),
            pltpu.VMEM((CELLS, PAD), bf16),
            pltpu.VMEM((CELLS, PAD), bf16),
            ring, ring, slab, slab, slab, slab, ring, ring,
            pltpu.VMEM((3 * 2 * 16 * 8, 128), f32),
            pltpu.VMEM((2, LAYERS, 4, 8, 128), f32),
            pltpu.VMEM((2, 8, 8, 128), f32),
            pltpu.VMEM((2, 2, 16, CELLS), f32),
            pltpu.VMEM((2, 16, 128), f32),
            pltpu.VMEM((2, 16, 128), f32),
            pltpu.VMEM((6, 16, CELLS), f32),
            dma((10,)), dma((4,)), dma((4,)), dma((4,)), dma((4,)), dma((2,)), dma((2,)),
        ],
        compiler_params=pltpu.CompilerParams(
            collective_id=0, has_side_effects=True, vmem_limit_bytes=60 * 1024 * 1024
        ),
        cost_estimate=pl.CostEstimate(flops=10**9, bytes_accessed=5 * 10**6, transcendentals=0),
        name="fields",
    )(polar, azimuth, saturation, anisotropy, stiffness, coupling, *transforms())


def solution(mesh):
    placed = (
        P("layer", "plane", None),
        P("layer", "plane", None),
        P("layer", "plane", None),
        P("layer", "plane", None),
        P("layer"),
        P(),
    )
    return jax.shard_map(
        body,
        mesh=mesh,
        in_specs=placed,
        out_specs=(P("layer", None, "plane", None), P("layer", None, "plane", None)),
        check_vma=False,
    )
```

```python
import functools
import math

import jax
import jax.numpy as jnp
import ml_dtypes
import numpy as np
from jax import lax
from jax.experimental import pallas as pl
from jax.experimental.pallas import tpu as pltpu
from jax.sharding import PartitionSpec as P

side_length = 512.0
spacing = 1.2
damping = 0.1
time_step = 0.1

CELLS = 512
PAD = 2 * CELLS
LAYERS = 16
RING = 16
SLAB = 32
MESH = pl.DeviceIdType.MESH
AWAY = [8, 7, 9, 6, 10, 5, 11, 4, 12, 3, 13, 2, 14, 1, 15]
FAR = [(a, b, dy) for a in range(2) for b in range(2) for dy in range(4)]
FAR.sort(key=lambda far: -((1 if far[1] else 2 * far[0]) + (0, 1, 2, 1)[far[2]]))
f32 = jnp.float32
bf16 = jnp.bfloat16


def halves(table):
    high = table.astype(ml_dtypes.bfloat16)
    low = (table - high.astype(np.float64)).astype(ml_dtypes.bfloat16)
    return high, low


@functools.lru_cache(None)
def transforms():
    column = np.arange(PAD)
    pair, core, part = column // 128, column // 64 % 2, column // 32 % 2
    wave = (2 * pair + column % 2) * SLAB + core * 16 + column // 2 % 16
    place = np.arange(CELLS)
    angle = (place[:, None] * wave[None, :] % PAD) * (2.0 * np.pi / PAD)
    along_y = np.where(part[None, :] == 0, np.cos(angle), np.sin(angle))
    alternating = np.where(place % 2 == 0, 1.0, -1.0)
    along_y[:, (wave == 0) & (part == 1)] = alternating[:, None]
    row = np.arange(CELLS)
    x = row // 256 * 256 + row % 16 * 16 + row // 128 % 2 * 8 + row // 64 % 2 * 4 + row // 16 % 4
    angle = (x[:, None] * np.arange(CELLS)[None, :] % PAD) * (2.0 * np.pi / PAD)
    sine = np.sin(angle)
    sine[:, 0] = np.where(x % 2 == 0, 1.0, -1.0)
    along_x = np.concatenate([np.cos(angle), sine], 1)
    return halves(along_y) + halves(along_x)


def polynomial(x, coefficients):
    total = jnp.full_like(x, coefficients[-1])
    for c in coefficients[-2::-1]:
        total = total * x + c
    return total


SIN = [(-1.0) ** n / math.factorial(2 * n + 1) for n in range(7)]
COS = [(-1.0) ** n / math.factorial(2 * n) for n in range(8)]
SINH = [1.0 / math.factorial(2 * n + 1) for n in range(11)]


def sin_cos(x):
    square = x * x
    return x * polynomial(square, SIN), polynomial(square, COS)


def unit_moment(polar, azimuth):
    sin_p, cos_p = sin_cos(polar)
    s, c = sin_cos(0.5 * azimuth)
    return sin_p * (1.0 - 2.0 * s * s), sin_p * (2.0 * s * c), cos_p


def product(left, high_ref, low_ref, transposed):
    high = left.astype(bf16)
    low = (left - high.astype(f32)).astype(bf16)
    rows = left.shape[0]
    dims = (((1,), (1 if transposed else 0,)), ((), ()))
    both = lax.dot_general(
        jnp.concatenate([high, low], 0), high_ref[...], dims, preferred_element_type=f32
    )
    rest = lax.dot_general(high, low_ref[...], dims, preferred_element_type=f32)
    return both[:rows] + both[rows:] + rest


def even_lanes():
    return lax.broadcasted_iota(jnp.int32, (8, 128), 1) % 2 == 0


def low_lanes(rows):
    return lax.broadcasted_iota(jnp.int32, (rows, 128), 1) < 64


def half_turn(x):
    return pltpu.roll(pltpu.roll(x, 64, 1), 4, 0)


def forward_y(m, saturation, wyh, wyl, s1):
    rows = [m[c][8 * h : 8 * h + 8] * saturation[8 * h : 8 * h + 8] for h in range(2) for c in range(3)]
    y = product(jnp.concatenate(rows, 0), wyh, wyl, False)
    even, low = even_lanes(), low_lanes(8)
    for c in range(3):
        for p in range(8):
            upper = y[8 * c : 8 * c + 8, 128 * p : 128 * p + 128]
            lower = y[24 + 8 * c : 32 + 8 * c, 128 * p : 128 * p + 128]
            first = jnp.where(even, upper, pltpu.roll(lower, 1, 1))
            second = jnp.where(even, pltpu.roll(upper, 127, 1), lower)
            for z, tile in ((2 * p, first), (2 * p + 1, second)):
                turned = half_turn(tile)
                s1[pl.ds(z * 12 + c * 4, 4), :] = jnp.where(low, tile, turned)[:4]
                s1[pl.ds(192 + z * 12 + c * 4, 4), :] = jnp.where(low, turned, tile)[4:]


def turn_in(k, r1, s2):
    for c in range(3):
        x = jnp.concatenate([r1[pl.ds(k * 192 + c * 4 + r, 16, stride=12), :] for r in range(4)], 0)
        block = jnp.concatenate([x, pltpu.roll(x, 64, 1)], 0).T
        for b in range(2):
            s2[pl.ds(k * 192 + 2 * c + b, 32, stride=6), :] = block[32 * b : 32 * b + 32]


def spectral_tables(fy, tb):
    sub = lax.broadcasted_iota(jnp.int32, (8, 128), 0)
    fx = sub % 4 * 128 + lax.broadcasted_iota(jnp.int32, (8, 128), 1)
    second = sub // 4 == 1
    sign = jnp.where(second, 1.0, -1.0)
    edge_x = fx == 0
    edge_y = jnp.full((8, 128), fy) == 0
    for v in range(2):
        sine_y = second if v == 0 else jnp.logical_not(second)
        high_x = jnp.logical_and(edge_x, second)
        high_y = jnp.logical_and(edge_y, sine_y)
        wave_x = jnp.where(high_x, CELLS, fx).astype(f32) * (math.pi / side_length)
        wave_y = jnp.where(high_y, CELLS, fy).astype(f32) * (math.pi / side_length)
        k = jnp.sqrt(wave_x * wave_x + wave_y * wave_y)
        nonzero = k > 0.0
        safe = jnp.where(nonzero, k, 1.0)
        inverse = 1.0 / safe
        half = 0.5 * safe
        ratio = polynomial(half * half, SINH)
        self_part = jnp.where(nonzero, jnp.exp(-half) * ratio, 1.0)
        mutual = jnp.where(nonzero, half * ratio * ratio, 0.0)
        weight = jnp.where(edge_x, 1.0, 2.0) * jnp.where(edge_y, 1.0, 2.0) * (1.0 / (PAD * PAD))
        ux, uy = wave_x * inverse, wave_y * inverse
        tb[v, 0] = jnp.exp(-spacing * k)
        tb[v, 1] = weight * (1.0 - self_part)
        tb[v, 2] = weight * mutual
        tb[v, 3] = weight * self_part
        tb[v, 4] = jnp.where(edge_x, 0.0, sign * ux)
        tb[v, 5] = jnp.where(edge_y, 0.0, sign * uy)
        tb[v, 6] = jnp.where(high_x, ux, 0.0)
        tb[v, 7] = jnp.where(high_y, uy, 0.0)


ORDER = [(0, 0), (1, 1), (0, 1), (1, 0)]
ORDER_X = [(1, 1), (0, 0), (1, 0), (0, 1)]


def tile_row(c, tg, cls, lb):
    return ((c * 2 + tg) * 16 + cls * 4 + lb) * 8


def transform_x(r2, wxh, wxl, zs):
    columns = []
    for x_lo in range(2):
        for h in range(2):
            parts = [r2[pl.ds(x_lo * 12 + h * 6 + q, 16, stride=24), :] for q in range(6)]
            columns.append(jnp.concatenate(parts, 0))
    z = product(jnp.concatenate(columns, 1), wxh, wxl, False)
    for c in range(3):
        for cls, (a, b) in enumerate(ORDER_X if c == 0 else ORDER):
            for tg in range(2):
                for lb in range(4):
                    row = (2 * c + b) * 16 + tg * 8
                    lane = a * 512 + lb * 128
                    zs[pl.ds(tile_row(c, tg, cls, lb), 8), :] = z[row : row + 8, lane : lane + 128]


def couple(zs, tb, ws):
    def at(c, t, v):
        return pl.ds(tile_row(c, t // 8, 2 * v, 0) + t % 8, 8, stride=8)

    for v in range(2):
        other = 1 - v
        decay, direct, mutual = tb[v, 0], tb[v, 1], tb[v, 2]
        ux, uy, lone_x, lone_y = tb[v, 4], tb[v, 5], tb[v, 6], tb[v, 7]
        if v == 1:
            uy = -uy
        carry = jnp.zeros((8, 128), f32)
        carry_lone = jnp.zeros((8, 128), f32)
        for t in range(LAYERS):
            r = ux * zs[at(0, t, other), :] + uy * zs[at(1, t, other), :]
            lone = lone_x * pltpu.roll(zs[at(0, t, v), :], 4, 0) + lone_y * zs[at(1, t, v), :]
            ws[v, t, 0] = r
            ws[v, t, 1] = lone
            ws[v, t, 2] = carry
            ws[v, t, 3] = carry_lone
            carry = decay * (carry + (zs[at(2, t, v), :] + r))
            carry_lone = decay * (carry_lone + lone)
    for v in range(2):
        decay, direct, mutual = tb[v, 0], tb[v, 1], tb[v, 2]
        carry = jnp.zeros((8, 128), f32)
        carry_lone = jnp.zeros((8, 128), f32)
        for t in range(LAYERS - 1, -1, -1):
            r, lone = ws[v, t, 0], ws[v, t, 1]
            below, below_lone = ws[v, t, 2], ws[v, t, 3]
            z = zs[at(2, t, v), :]
            ws[v, t, 0] = direct * r + mutual * (below + carry)
            ws[v, t, 1] = direct * lone + mutual * (below_lone + carry_lone)
            zs[at(2, t, v), :] = mutual * (below - carry) - tb[v, 3] * z
            carry = decay * (carry + (r - z))
            carry_lone = decay * (carry_lone + lone)
    for v in range(2):
        other = 1 - v
        ux, uy, lone_x, lone_y = tb[other, 4], tb[v, 5], tb[v, 6], tb[v, 7]
        if v == 1:
            uy = -uy
        for t in range(LAYERS):
            h, lone = ws[other, t, 0], ws[v, t, 1]
            zs[at(0, t, v), :] = -ux * h - pltpu.roll(lone_x * lone, 4, 0)
            zs[at(1, t, v), :] = uy * h - lone_y * lone


def return_x(zs, wxh, wxl, s3):
    rows = []
    for c in range(3):
        order = ORDER_X if c == 0 else ORDER
        for b in range(2):
            for tg in range(2):
                lanes = [
                    zs[pl.ds(tile_row(c, tg, order.index((a, b)), lb), 8), :] for a in range(2) for lb in range(4)
                ]
                rows.append(jnp.concatenate(lanes, 1))
    out = product(jnp.concatenate(rows, 0), wxh, wxl, True)
    for x_lo in range(2):
        for h in range(2):
            lane = (x_lo * 2 + h) * 128
            for q in range(6):
                s3[pl.ds(x_lo * 12 + h * 6 + q, 16, stride=24), :] = out[16 * q : 16 * q + 16, lane : lane + 128]


def turn_out(k, r3, s4):
    low = low_lanes(64)
    for c in range(3):
        parts = [r3[pl.ds(k * 192 + 2 * c + b, 32, stride=6), :] for b in range(2)]
        block = jnp.concatenate(parts + parts, 0).T
        block = jnp.where(low, block[:64], block[64:])
        for r in range(4):
            s4[pl.ds(k * 192 + c * 4 + r, 16, stride=12), :] = block[16 * r : 16 * r + 16]


def inverse_y(r4, wyh, wyl):
    even = even_lanes()
    kept = low_lanes(8) == (lax.broadcasted_iota(jnp.int32, (8, 128), 0) < 4)

    def tile(z, c):
        both = jnp.concatenate([r4[pl.ds(k * 192 + z * 12 + c * 4, 4), :] for k in range(2)], 0)
        return jnp.where(kept, both, half_turn(both))

    upper, lower = [], []
    for c in range(3):
        up, low = [], []
        for p in range(8):
            first, second = tile(2 * p, c), tile(2 * p + 1, c)
            up.append(jnp.where(even, first, pltpu.roll(second, 1, 1)))
            low.append(jnp.where(even, pltpu.roll(first, 127, 1), second))
        upper.append(jnp.concatenate(up, 1))
        lower.append(jnp.concatenate(low, 1))
    out = product(jnp.concatenate(upper + lower, 0), wyh, wyl, True)
    return [jnp.concatenate([out[8 * c : 8 * c + 8], out[24 + 8 * c : 32 + 8 * c]], 0) for c in range(3)]


def cross_product(a, b):
    return (a[1] * b[2] - a[2] * b[1], a[2] * b[0] - a[0] * b[2], a[0] * b[1] - a[1] * b[0])


def other_fields(m, first_row, last_row, lower_m, upper_m, stiffness, lower_link, upper_link, anisotropy):
    lane = lax.broadcasted_iota(jnp.int32, (16, 512), 1)
    fields = []
    for c in range(3):
        beside = jnp.concatenate([first_row[c], m[c][:15]], 0) + jnp.concatenate([m[c][1:], last_row[c]], 0)
        beside = beside + jnp.where(lane == 0, 0.0, pltpu.roll(m[c], 1, 1))
        beside = beside + jnp.where(lane == 511, 0.0, pltpu.roll(m[c], 511, 1))
        fields.append(stiffness * beside + lower_link * lower_m[c] + upper_link * upper_m[c])
    fields[2] = fields[2] + anisotropy * m[2]
    return fields


def step(m, field):
    first = cross_product(m, field)
    second = cross_product(m, first)
    scale = -time_step / (1.0 + damping * damping)
    stepped = [m[c] + scale * (first[c] + damping * second[c]) for c in range(3)]
    inverse = lax.rsqrt(stepped[0] * stepped[0] + stepped[1] * stepped[1] + stepped[2] * stepped[2])
    return [s * inverse for s in stepped]


def kernel(
    polar_any, azimuth_any, saturation_any, anisotropy_any, stiffness_any, coupling_any,
    wyh_any, wyl_any, wxh_any, wxl_any,
    field_out, moment_out,
    polar, azimuth, saturation, anisotropy, stiffness, coupling,
    wyh, wyl, wxh, wxl, s1, r1, s2, r2, s3, r3, s4, r4, zs, ws, tb, near, edge_out, edge_in, rest,
    load_sem, send_sem, recv_sem, near_send, near_recv, edge_send, edge_recv,
):
    t = lax.axis_index("layer")
    p = lax.axis_index("plane")
    z = lax.rem(p, RING)
    x_lo = lax.div(p, RING)
    core = lax.rem(t, 2)
    y = lax.rem(lax.div(t, 2), 4)
    x_hi = lax.div(t, 8)
    source = t * 2 + x_lo
    owner = core * 16 + lax.div(t, 2) * 2 + x_lo

    loads = [
        pltpu.make_async_copy(src, dst, load_sem.at[i])
        for i, (src, dst) in enumerate([
            (polar_any, polar), (azimuth_any, azimuth), (saturation_any, saturation), (wyh_any, wyh), (wyl_any, wyl),
            (anisotropy_any, anisotropy), (stiffness_any, stiffness), (coupling_any, coupling),
            (wxh_any, wxh), (wxl_any, wxl),
        ])
    ]
    for load in loads:
        load.start()

    def ring_device(away):
        there = lax.rem(z + away, RING)
        return there, (t, x_lo * RING + there)

    def slab_device(far, there_core):
        a, b, dy = far
        there_x = lax.rem(x_lo + b, 2)
        pair = lax.rem(x_hi + a, 2) * 4 + lax.rem(y + dy, 4)
        there_t = pair * 2 + there_core
        return there_t * 2 + there_x, there_core * 16 + pair * 2 + there_x, (there_t, there_x * RING + z)

    next_plane = (t, lax.rem(p + 1, 2 * RING))
    last_plane = (t, lax.rem(p + 2 * RING - 1, 2 * RING))
    next_layer = (lax.rem(t + 1, LAYERS), p)
    last_layer = (lax.rem(t + LAYERS - 1, LAYERS), p)

    barrier = pltpu.get_barrier_semaphore()

    def greet(there):
        pl.semaphore_signal(barrier, inc=1, device_id=there, device_id_type=MESH)

    for away in AWAY:
        greet(ring_device(away)[1])
    for far in FAR:
        greet(slab_device(far, 1 - core)[2])
        if any(far):
            greet(slab_device(far, core)[2])
    for there in (next_plane, last_plane):
        greet(there)

    loads[0].wait()
    loads[1].wait()
    m = unit_moment(polar[0], azimuth[0])
    edge_out[...] = jnp.zeros((2, 16, 128), f32)
    for side, row in enumerate((0, 15)):
        for c in range(3):
            for lb in range(4):
                edge_out[side, c * 4 + lb : c * 4 + lb + 1, :] = m[c][row : row + 1, 128 * lb : 128 * lb + 128]
    for load in loads[2:5]:
        load.wait()
    forward_y(m, saturation[0], wyh, wyl, s1)

    pl.semaphore_wait(barrier, RING - 1 + SLAB - 1 + 2)

    def remote(src, dst, sem, there):
        return pltpu.make_async_remote_copy(
            src_ref=src, dst_ref=dst, send_sem=sem[0], recv_sem=sem[1], device_id=there, device_id_type=MESH
        )

    def rows_of(ref, i):
        return ref.at[pl.ds(pl.multiple_of(i * 12, 4), 12)]

    def ring_send(src, dst, n, k, arrival):
        for away in AWAY:
            there, device = ring_device(away)
            sems = (send_sem.at[n], recv_sem.at[arrival])
            remote(rows_of(src, k * 16 + there), rows_of(dst, k * 16 + z), sems, device).start()
        pltpu.make_async_copy(rows_of(src, k * 16 + z), rows_of(dst, k * 16 + z), recv_sem.at[arrival]).start()

    def slab_send(k):
        sems = (send_sem.at[1], recv_sem.at[2])
        for far in FAR:
            _, there, device = slab_device(far, k)
            if any(far):
                remote(rows_of(s2, there), rows_of(r2, source), sems, device).start()
            else:

                @pl.when(core == k)
                def _():
                    pltpu.make_async_copy(rows_of(s2, owner), rows_of(r2, source), recv_sem.at[2]).start()

                @pl.when(core != k)
                def _():
                    remote(rows_of(s2, there), rows_of(r2, source), sems, device).start()

    def slab_return():
        sems = (send_sem.at[2], recv_sem.at[3 + core])
        for far in FAR:
            for there_core in (core, 1 - core):
                there, _, device = slab_device(far, there_core)
                if any(far) or there_core is not core:
                    remote(rows_of(s3, there), rows_of(r3, owner), sems, device).start()
        pltpu.make_async_copy(rows_of(s3, source), rows_of(r3, owner), recv_sem.at[3 + core]).start()

    def received(dst, n, rows=192):
        part = dst.at[pl.ds(0, rows)]
        pltpu.make_async_copy(part, part, recv_sem.at[n]).wait()

    for k in range(2):
        ring_send(s1, r1, 0, k, k)
    sides = []
    for i, (ref, side, there) in enumerate(
        [(polar, 0, next_layer), (azimuth, 0, next_layer), (polar, 1, last_layer), (azimuth, 1, last_layer)]
    ):
        sides.append(remote(ref.at[0], near.at[side, i % 2], (near_send.at[i], near_recv.at[i]), there))
    for side, there in ((0, last_plane), (1, next_plane)):
        sides.append(
            remote(edge_out.at[side], edge_in.at[1 - side], (edge_send.at[side], edge_recv.at[side]), there)
        )
    for copy in sides:
        copy.start()

    for load in loads[5:]:
        load.wait()
    spectral_tables(z * SLAB + owner, tb)
    for k in range(2):
        received(r1, k)
        turn_in(k, r1, s2)
        slab_send(k)
    for copy in sides:
        copy.wait_recv()
    lower_m = unit_moment(near[0, 0], near[0, 1])
    upper_m = unit_moment(near[1, 0], near[1, 1])
    lower_link = jnp.where(t > 0, coupling[jnp.maximum(t - 1, 0)], 0.0)
    upper_link = jnp.where(t < LAYERS - 1, coupling[jnp.minimum(t, LAYERS - 2)], 0.0)

    def edge_row(side, present):
        rows = []
        for c in range(3):
            lanes = [edge_in[side, c * 4 + lb : c * 4 + lb + 1, :] for lb in range(4)]
            rows.append(jnp.where(present, jnp.concatenate(lanes, 1), 0.0))
        return rows

    m = unit_moment(polar[0], azimuth[0])
    fields = other_fields(
        m, edge_row(0, p > 0), edge_row(1, p < 2 * RING - 1), lower_m, upper_m,
        stiffness[0], lower_link, upper_link, anisotropy[0],
    )
    for c in range(3):
        rest[c] = fields[c]
        rest[3 + c] = m[c]

    received(r2, 2, 384)
    transform_x(r2, wxh, wxl, zs)
    couple(zs, tb, ws)
    return_x(zs, wxh, wxl, s3)
    slab_return()
    for k in range(2):
        received(r3, 3 + k)
        turn_out(k, r3, s4)
        ring_send(s4, r4, 3, k, 5 + k)
    received(r4, 5)
    received(r4, 6)
    demag = inverse_y(r4, wyh, wyl)
    m = [rest[3 + c] for c in range(3)]
    field = [demag[c] + rest[c] for c in range(3)]
    moment = step(m, field)
    for c in range(3):
        field_out[0, c] = field[c]
        moment_out[0, c] = moment[c]

    for copy in sides:
        copy.wait_send()
    for n, rows in ((0, 360), (1, 372), (2, 372), (3, 360)):
        part = s1.at[pl.ds(0, rows)]
        pltpu.make_async_copy(part, part, send_sem.at[n]).wait()


def body(polar, azimuth, saturation, anisotropy, stiffness, coupling):
    vmem = pl.BlockSpec(memory_space=pltpu.VMEM)
    hbm = pl.BlockSpec(memory_space=pltpu.HBM)
    out = jax.ShapeDtypeStruct((1, 3, 16, CELLS), f32)
    dma = pltpu.SemaphoreType.DMA
    block = pltpu.VMEM((SLAB * 12, 128), f32)
    row_block = pltpu.VMEM((1, 16, CELLS), f32)
    return pl.pallas_call(
        kernel,
        out_shape=(out, out),
        in_specs=[hbm] * 10,
        out_specs=(vmem, vmem),
        scratch_shapes=[
            row_block, row_block, row_block, row_block,
            pltpu.SMEM((1,), f32), pltpu.SMEM((LAYERS - 1,), f32),
            pltpu.VMEM((CELLS, PAD), bf16),
            pltpu.VMEM((CELLS, PAD), bf16),
            pltpu.VMEM((CELLS, PAD), bf16),
            pltpu.VMEM((CELLS, PAD), bf16),
            block, block, block, block, block, block, block, block,
            pltpu.VMEM((3 * 2 * 16 * 8, 128), f32),
            pltpu.VMEM((2, LAYERS, 4, 8, 128), f32),
            pltpu.VMEM((2, 8, 8, 128), f32),
            pltpu.VMEM((2, 2, 16, CELLS), f32),
            pltpu.VMEM((2, 16, 128), f32),
            pltpu.VMEM((2, 16, 128), f32),
            pltpu.VMEM((6, 16, CELLS), f32),
            dma((10,)), dma((4,)), dma((7,)), dma((4,)), dma((4,)), dma((2,)), dma((2,)),
        ],
        compiler_params=pltpu.CompilerParams(
            collective_id=0, has_side_effects=True, vmem_limit_bytes=60 * 1024 * 1024
        ),
        cost_estimate=pl.CostEstimate(flops=10**9, bytes_accessed=5 * 10**6, transcendentals=0),
        name="fields",
    )(polar, azimuth, saturation, anisotropy, stiffness, coupling, *transforms())


def solution(mesh):
    placed = (
        P("layer", "plane", None),
        P("layer", "plane", None),
        P("layer", "plane", None),
        P("layer", "plane", None),
        P("layer"),
        P(),
    )
    return jax.shard_map(
        body,
        mesh=mesh,
        in_specs=placed,
        out_specs=(P("layer", None, "plane", None), P("layer", None, "plane", None)),
        check_vma=False,
    )
```

```python
import functools
import math

import jax
import jax.numpy as jnp
import ml_dtypes
import numpy as np
from jax import lax
from jax.experimental import pallas as pl
from jax.experimental.pallas import tpu as pltpu
from jax.sharding import PartitionSpec as P

side_length = 512.0
spacing = 1.2
damping = 0.1
time_step = 0.1

CELLS = 512
PAD = 2 * CELLS
LAYERS = 16
RING = 16
SLAB = 32
MESH = pl.DeviceIdType.MESH
AWAY = [8, 7, 9, 6, 10, 5, 11, 4, 12, 3, 13, 2, 14, 1, 15]
FAR = [(a, b, dy) for a in range(2) for b in range(2) for dy in range(4)]
FAR.sort(key=lambda far: -((1 if far[1] else 2 * far[0]) + (0, 1, 2, 1)[far[2]]))
f32 = jnp.float32
bf16 = jnp.bfloat16


def halves(table):
    high = table.astype(ml_dtypes.bfloat16)
    low = (table - high.astype(np.float64)).astype(ml_dtypes.bfloat16)
    return high, low


@functools.lru_cache(None)
def transforms():
    column = np.arange(PAD)
    core, part = column // 512, column // 32 % 2
    wave = (column // 64 % 8 * 2 + column % 2) * SLAB + core * 16 + column // 2 % 16
    place = np.arange(CELLS)
    angle = (place[:, None] * wave[None, :] % PAD) * (2.0 * np.pi / PAD)
    along_y = np.where(part[None, :] == 0, np.cos(angle), np.sin(angle))
    alternating = np.where(place % 2 == 0, 1.0, -1.0)
    along_y[:, (wave == 0) & (part == 1)] = alternating[:, None]
    row = np.arange(CELLS)
    x = row // 256 * 256 + row % 16 * 16 + row // 128 % 2 * 8 + row // 64 % 2 * 4 + row // 16 % 4
    angle = (x[:, None] * np.arange(CELLS)[None, :] % PAD) * (2.0 * np.pi / PAD)
    sine = np.sin(angle)
    sine[:, 0] = np.where(x % 2 == 0, 1.0, -1.0)
    along_x = np.concatenate([np.cos(angle), sine], 1)
    return halves(along_y) + halves(along_x)


def polynomial(x, coefficients):
    total = jnp.full_like(x, coefficients[-1])
    for c in coefficients[-2::-1]:
        total = total * x + c
    return total


SIN = [(-1.0) ** n / math.factorial(2 * n + 1) for n in range(7)]
COS = [(-1.0) ** n / math.factorial(2 * n) for n in range(8)]
SINH = [1.0 / math.factorial(2 * n + 1) for n in range(11)]


def sin_cos(x):
    square = x * x
    return x * polynomial(square, SIN), polynomial(square, COS)


def unit_moment(polar, azimuth):
    sin_p, cos_p = sin_cos(polar)
    s, c = sin_cos(0.5 * azimuth)
    return sin_p * (1.0 - 2.0 * s * s), sin_p * (2.0 * s * c), cos_p


def product(left, high, low, transposed):
    left_high = left.astype(bf16)
    left_low = (left - left_high.astype(f32)).astype(bf16)
    rows = left.shape[0]
    dims = (((1,), (1 if transposed else 0,)), ((), ()))
    both = lax.dot_general(
        jnp.concatenate([left_high, left_low], 0), high, dims, preferred_element_type=f32
    )
    rest = lax.dot_general(left_high, low, dims, preferred_element_type=f32)
    return both[:rows] + both[rows:] + rest


def even_lanes():
    return lax.broadcasted_iota(jnp.int32, (8, 128), 1) % 2 == 0


def low_lanes(rows):
    return lax.broadcasted_iota(jnp.int32, (rows, 128), 1) < 64


def half_turn(x):
    return pltpu.roll(pltpu.roll(x, 64, 1), 4, 0)


def forward_y(m, saturation, wyh, wyl, s1):
    rows = [m[c][8 * h : 8 * h + 8] * saturation[8 * h : 8 * h + 8] for h in range(2) for c in range(3)]
    y = product(jnp.concatenate(rows, 0), wyh[...], wyl[...], False)
    even, low = even_lanes(), low_lanes(8)
    for c in range(3):
        for p in range(8):
            upper = y[8 * c : 8 * c + 8, 128 * p : 128 * p + 128]
            lower = y[24 + 8 * c : 32 + 8 * c, 128 * p : 128 * p + 128]
            first = jnp.where(even, upper, pltpu.roll(lower, 1, 1))
            second = jnp.where(even, pltpu.roll(upper, 127, 1), lower)
            for z, tile in ((p % 4 * 4, first), (p % 4 * 4 + 1, second)):
                turned = half_turn(tile)
                row = (p // 4 * 16 + z) * 12 + c * 4
                s1[pl.ds(row, 4), :] = jnp.where(low, tile, turned)[:4]
                s1[pl.ds(row + 24, 4), :] = jnp.where(low, turned, tile)[4:]


def turn_in(k, r1, s2):
    for c in range(3):
        x = jnp.concatenate([r1[pl.ds(k * 192 + c * 4 + r, 16, stride=12), :] for r in range(4)], 0)
        block = jnp.concatenate([x, pltpu.roll(x, 64, 1)], 0).T
        for b in range(2):
            s2[pl.ds(k * 192 + 2 * c + b, 32, stride=6), :] = block[32 * b : 32 * b + 32]


def spectral_tables(fy, tb):
    sub = lax.broadcasted_iota(jnp.int32, (8, 128), 0)
    fx = sub % 4 * 128 + lax.broadcasted_iota(jnp.int32, (8, 128), 1)
    second = sub // 4 == 1
    sign = jnp.where(second, 1.0, -1.0)
    edge_x = fx == 0
    edge_y = jnp.full((8, 128), fy) == 0
    for v in range(2):
        sine_y = second if v == 0 else jnp.logical_not(second)
        high_x = jnp.logical_and(edge_x, second)
        high_y = jnp.logical_and(edge_y, sine_y)
        wave_x = jnp.where(high_x, CELLS, fx).astype(f32) * (math.pi / side_length)
        wave_y = jnp.where(high_y, CELLS, fy).astype(f32) * (math.pi / side_length)
        k = jnp.sqrt(wave_x * wave_x + wave_y * wave_y)
        nonzero = k > 0.0
        safe = jnp.where(nonzero, k, 1.0)
        inverse = 1.0 / safe
        half = 0.5 * safe
        ratio = polynomial(half * half, SINH)
        self_part = jnp.where(nonzero, jnp.exp(-half) * ratio, 1.0)
        mutual = jnp.where(nonzero, half * ratio * ratio, 0.0)
        weight = jnp.where(edge_x, 1.0, 2.0) * jnp.where(edge_y, 1.0, 2.0) * (1.0 / (PAD * PAD))
        ux, uy = wave_x * inverse, wave_y * inverse
        tb[v, 0] = jnp.exp(-spacing * k)
        tb[v, 1] = weight * (1.0 - self_part)
        tb[v, 2] = weight * mutual
        tb[v, 3] = weight * self_part
        tb[v, 4] = jnp.where(edge_x, 0.0, sign * ux)
        tb[v, 5] = jnp.where(edge_y, 0.0, sign * uy)
        tb[v, 6] = jnp.where(high_x, ux, 0.0)
        tb[v, 7] = jnp.where(high_y, uy, 0.0)


ORDER = [(0, 0), (1, 1), (0, 1), (1, 0)]
ORDER_X = [(1, 1), (0, 0), (1, 0), (0, 1)]


def tile_row(c, tg, cls, lb):
    return ((c * 2 + tg) * 16 + cls * 4 + lb) * 8


def transform_x(r2, wxh, wxl, zs):
    columns = []
    for x_lo in range(2):
        for h in range(2):
            parts = [r2[pl.ds(x_lo * 12 + h * 6 + q, 16, stride=24), :] for q in range(6)]
            columns.append(jnp.concatenate(parts, 0))
    z = product(jnp.concatenate(columns, 1), wxh[...], wxl[...], False)
    for c in range(3):
        for cls, (a, b) in enumerate(ORDER_X if c == 0 else ORDER):
            for tg in range(2):
                for lb in range(4):
                    row = (2 * c + b) * 16 + tg * 8
                    lane = a * 512 + lb * 128
                    zs[pl.ds(tile_row(c, tg, cls, lb), 8), :] = z[row : row + 8, lane : lane + 128]


def couple(zs, tb, ws):
    def at(c, t, v):
        return pl.ds(tile_row(c, t // 8, 2 * v, 0) + t % 8, 8, stride=8)

    for v in range(2):
        other = 1 - v
        decay, direct, mutual = tb[v, 0], tb[v, 1], tb[v, 2]
        ux, uy, lone_x, lone_y = tb[v, 4], tb[v, 5], tb[v, 6], tb[v, 7]
        if v == 1:
            uy = -uy
        carry = jnp.zeros((8, 128), f32)
        carry_lone = jnp.zeros((8, 128), f32)
        for t in range(LAYERS):
            r = ux * zs[at(0, t, other), :] + uy * zs[at(1, t, other), :]
            lone = lone_x * pltpu.roll(zs[at(0, t, v), :], 4, 0) + lone_y * zs[at(1, t, v), :]
            ws[v, t, 0] = r
            ws[v, t, 1] = lone
            ws[v, t, 2] = carry
            ws[v, t, 3] = carry_lone
            carry = decay * (carry + (zs[at(2, t, v), :] + r))
            carry_lone = decay * (carry_lone + lone)
    for v in range(2):
        decay, direct, mutual = tb[v, 0], tb[v, 1], tb[v, 2]
        carry = jnp.zeros((8, 128), f32)
        carry_lone = jnp.zeros((8, 128), f32)
        for t in range(LAYERS - 1, -1, -1):
            r, lone = ws[v, t, 0], ws[v, t, 1]
            below, below_lone = ws[v, t, 2], ws[v, t, 3]
            z = zs[at(2, t, v), :]
            ws[v, t, 0] = direct * r + mutual * (below + carry)
            ws[v, t, 1] = direct * lone + mutual * (below_lone + carry_lone)
            zs[at(2, t, v), :] = mutual * (below - carry) - tb[v, 3] * z
            carry = decay * (carry + (r - z))
            carry_lone = decay * (carry_lone + lone)
    for v in range(2):
        other = 1 - v
        ux, uy, lone_x, lone_y = tb[other, 4], tb[v, 5], tb[v, 6], tb[v, 7]
        if v == 1:
            uy = -uy
        for t in range(LAYERS):
            h, lone = ws[other, t, 0], ws[v, t, 1]
            zs[at(0, t, v), :] = -ux * h - pltpu.roll(lone_x * lone, 4, 0)
            zs[at(1, t, v), :] = uy * h - lone_y * lone


def return_x(zs, wxh, wxl, s3):
    rows = []
    for c in range(3):
        order = ORDER_X if c == 0 else ORDER
        for b in range(2):
            for tg in range(2):
                lanes = [
                    zs[pl.ds(tile_row(c, tg, order.index((a, b)), lb), 8), :] for a in range(2) for lb in range(4)
                ]
                rows.append(jnp.concatenate(lanes, 1))
    out = product(jnp.concatenate(rows, 0), wxh[...], wxl[...], True)
    for x_lo in range(2):
        for h in range(2):
            lane = (x_lo * 2 + h) * 128
            for q in range(6):
                s3[pl.ds(x_lo * 12 + h * 6 + q, 16, stride=24), :] = out[16 * q : 16 * q + 16, lane : lane + 128]


def turn_out(k, r3, s4):
    low = low_lanes(64)
    for c in range(3):
        parts = [r3[pl.ds(k * 192 + 2 * c + b, 32, stride=6), :] for b in range(2)]
        block = jnp.concatenate(parts + parts, 0).T
        block = jnp.where(low, block[:64], block[64:])
        for r in range(4):
            s4[pl.ds(k * 192 + c * 4 + r, 16, stride=12), :] = block[16 * r : 16 * r + 16]


def inverse_y(k, r4, wyh, wyl):
    even = even_lanes()
    kept = low_lanes(8) == (lax.broadcasted_iota(jnp.int32, (8, 128), 0) < 4)

    def tile(z, c):
        row = k * 192 + z * 12 + c * 4
        both = jnp.concatenate([r4[pl.ds(row, 4), :], r4[pl.ds(row + 24, 4), :]], 0)
        return jnp.where(kept, both, half_turn(both))

    upper, lower = [], []
    for c in range(3):
        up, low = [], []
        for p in range(4):
            first, second = tile(4 * p, c), tile(4 * p + 1, c)
            up.append(jnp.where(even, first, pltpu.roll(second, 1, 1)))
            low.append(jnp.where(even, pltpu.roll(first, 127, 1), second))
        upper.append(jnp.concatenate(up, 1))
        lower.append(jnp.concatenate(low, 1))
    columns = slice(512 * k, 512 * k + 512)
    return product(jnp.concatenate(upper + lower, 0), wyh[:, columns], wyl[:, columns], True)


def cross_product(a, b):
    return (a[1] * b[2] - a[2] * b[1], a[2] * b[0] - a[0] * b[2], a[0] * b[1] - a[1] * b[0])


def other_fields(m, first_row, last_row, lower_m, upper_m, stiffness, lower_link, upper_link, anisotropy):
    lane = lax.broadcasted_iota(jnp.int32, (16, 512), 1)
    fields = []
    for c in range(3):
        beside = jnp.concatenate([first_row[c], m[c][:15]], 0) + jnp.concatenate([m[c][1:], last_row[c]], 0)
        beside = beside + jnp.where(lane == 0, 0.0, pltpu.roll(m[c], 1, 1))
        beside = beside + jnp.where(lane == 511, 0.0, pltpu.roll(m[c], 511, 1))
        fields.append(stiffness * beside + lower_link * lower_m[c] + upper_link * upper_m[c])
    fields[2] = fields[2] + anisotropy * m[2]
    return fields


def step(m, field):
    first = cross_product(m, field)
    second = cross_product(m, first)
    scale = -time_step / (1.0 + damping * damping)
    stepped = [m[c] + scale * (first[c] + damping * second[c]) for c in range(3)]
    inverse = lax.rsqrt(stepped[0] * stepped[0] + stepped[1] * stepped[1] + stepped[2] * stepped[2])
    return [s * inverse for s in stepped]


def kernel(
    polar_any, azimuth_any, saturation_any, anisotropy_any, stiffness_any, coupling_any,
    wyh_any, wyl_any, wxh_any, wxl_any,
    field_out, moment_out,
    polar, azimuth, saturation, anisotropy, stiffness, coupling,
    wyh, wyl, wxh, wxl, s1, r1, s2, r2, s3, r3, s4, r4, zs, ws, tb, near, edge_out, edge_in, rest,
    load_sem, send_sem, recv_sem, near_send, near_recv, edge_send, edge_recv,
):
    t = lax.axis_index("layer")
    p = lax.axis_index("plane")
    z = lax.rem(p, RING)
    x_lo = lax.div(p, RING)
    core = lax.rem(t, 2)
    y = lax.rem(lax.div(t, 2), 4)
    x_hi = lax.div(t, 8)
    source = t * 2 + x_lo
    owner = core * 16 + lax.div(t, 2) * 2 + x_lo

    loads = [
        pltpu.make_async_copy(src, dst, load_sem.at[i])
        for i, (src, dst) in enumerate([
            (polar_any, polar), (azimuth_any, azimuth), (saturation_any, saturation), (wyh_any, wyh), (wyl_any, wyl),
            (anisotropy_any, anisotropy), (stiffness_any, stiffness), (coupling_any, coupling),
            (wxh_any, wxh), (wxl_any, wxl),
        ])
    ]
    for load in loads:
        load.start()

    def ring_device(away):
        there = lax.rem(z + away, RING)
        return there, (t, x_lo * RING + there)

    def slab_device(far, there_core):
        a, b, dy = far
        there_x = lax.rem(x_lo + b, 2)
        pair = lax.rem(x_hi + a, 2) * 4 + lax.rem(y + dy, 4)
        there_t = pair * 2 + there_core
        return there_t * 2 + there_x, there_core * 16 + pair * 2 + there_x, (there_t, there_x * RING + z)

    next_plane = (t, lax.rem(p + 1, 2 * RING))
    last_plane = (t, lax.rem(p + 2 * RING - 1, 2 * RING))
    next_layer = (lax.rem(t + 1, LAYERS), p)
    last_layer = (lax.rem(t + LAYERS - 1, LAYERS), p)

    barrier = pltpu.get_barrier_semaphore()

    def greet(there):
        pl.semaphore_signal(barrier, inc=1, device_id=there, device_id_type=MESH)

    for away in AWAY:
        greet(ring_device(away)[1])
    for far in FAR:
        greet(slab_device(far, 1 - core)[2])
        if any(far):
            greet(slab_device(far, core)[2])
    for there in (next_plane, last_plane):
        greet(there)

    loads[0].wait()
    loads[1].wait()
    m = unit_moment(polar[0], azimuth[0])
    edge_out[...] = jnp.zeros((2, 16, 128), f32)
    for side, row in enumerate((0, 15)):
        for c in range(3):
            for lb in range(4):
                edge_out[side, c * 4 + lb : c * 4 + lb + 1, :] = m[c][row : row + 1, 128 * lb : 128 * lb + 128]
    for load in loads[2:5]:
        load.wait()
    forward_y(m, saturation[0], wyh, wyl, s1)

    pl.semaphore_wait(barrier, RING - 1 + SLAB - 1 + 2)

    def remote(src, dst, sem, there):
        return pltpu.make_async_remote_copy(
            src_ref=src, dst_ref=dst, send_sem=sem[0], recv_sem=sem[1], device_id=there, device_id_type=MESH
        )

    def rows_of(ref, i):
        return ref.at[pl.ds(pl.multiple_of(i * 12, 4), 12)]

    def ring_send(src, dst, n, k, arrival):
        for away in AWAY:
            there, device = ring_device(away)
            sems = (send_sem.at[n], recv_sem.at[arrival])
            remote(rows_of(src, k * 16 + there), rows_of(dst, k * 16 + z), sems, device).start()
        pltpu.make_async_copy(rows_of(src, k * 16 + z), rows_of(dst, k * 16 + z), recv_sem.at[arrival]).start()

    def slab_send(k):
        sems = (send_sem.at[1], recv_sem.at[2])
        for far in FAR:
            _, there, device = slab_device(far, k)
            if any(far):
                remote(rows_of(s2, there), rows_of(r2, source), sems, device).start()
            else:

                @pl.when(core == k)
                def _():
                    pltpu.make_async_copy(rows_of(s2, owner), rows_of(r2, source), recv_sem.at[2]).start()

                @pl.when(core != k)
                def _():
                    remote(rows_of(s2, there), rows_of(r2, source), sems, device).start()

    def slab_return():
        sems = (send_sem.at[2], recv_sem.at[3 + core])
        for far in FAR:
            for there_core in (core, 1 - core):
                there, _, device = slab_device(far, there_core)
                if any(far) or there_core is not core:
                    remote(rows_of(s3, there), rows_of(r3, owner), sems, device).start()
        pltpu.make_async_copy(rows_of(s3, source), rows_of(r3, owner), recv_sem.at[3 + core]).start()

    def received(dst, n, rows=192):
        part = dst.at[pl.ds(0, rows)]
        pltpu.make_async_copy(part, part, recv_sem.at[n]).wait()

    for k in range(2):
        ring_send(s1, r1, 0, k, k)
    sides = []
    for i, (ref, side, there) in enumerate(
        [(polar, 0, next_layer), (azimuth, 0, next_layer), (polar, 1, last_layer), (azimuth, 1, last_layer)]
    ):
        sides.append(remote(ref.at[0], near.at[side, i % 2], (near_send.at[i], near_recv.at[i]), there))
    for side, there in ((0, last_plane), (1, next_plane)):
        sides.append(
            remote(edge_out.at[side], edge_in.at[1 - side], (edge_send.at[side], edge_recv.at[side]), there)
        )
    for copy in sides:
        copy.start()

    for load in loads[5:]:
        load.wait()
    spectral_tables(z * SLAB + owner, tb)
    for k in range(2):
        received(r1, k)
        turn_in(k, r1, s2)
        slab_send(k)
    for copy in sides:
        copy.wait_recv()
    lower_m = unit_moment(near[0, 0], near[0, 1])
    upper_m = unit_moment(near[1, 0], near[1, 1])
    lower_link = jnp.where(t > 0, coupling[jnp.maximum(t - 1, 0)], 0.0)
    upper_link = jnp.where(t < LAYERS - 1, coupling[jnp.minimum(t, LAYERS - 2)], 0.0)

    def edge_row(side, present):
        rows = []
        for c in range(3):
            lanes = [edge_in[side, c * 4 + lb : c * 4 + lb + 1, :] for lb in range(4)]
            rows.append(jnp.where(present, jnp.concatenate(lanes, 1), 0.0))
        return rows

    m = unit_moment(polar[0], azimuth[0])
    fields = other_fields(
        m, edge_row(0, p > 0), edge_row(1, p < 2 * RING - 1), lower_m, upper_m,
        stiffness[0], lower_link, upper_link, anisotropy[0],
    )
    for c in range(3):
        rest[c] = fields[c]
        rest[3 + c] = m[c]

    received(r2, 2, 384)
    transform_x(r2, wxh, wxl, zs)
    couple(zs, tb, ws)
    return_x(zs, wxh, wxl, s3)
    slab_return()
    for k in range(2):
        received(r3, 3 + k)
        turn_out(k, r3, s4)
        ring_send(s4, r4, 3, k, 5 + k)
    received(r4, 5)
    demag = inverse_y(0, r4, wyh, wyl)
    received(r4, 6)
    demag = demag + inverse_y(1, r4, wyh, wyl)
    m = [rest[3 + c] for c in range(3)]
    field = [
        jnp.concatenate([demag[8 * c : 8 * c + 8], demag[24 + 8 * c : 32 + 8 * c]], 0) + rest[c] for c in range(3)
    ]
    moment = step(m, field)
    for c in range(3):
        field_out[0, c] = field[c]
        moment_out[0, c] = moment[c]

    for copy in sides:
        copy.wait_send()
    for n, rows in ((0, 360), (1, 372), (2, 372), (3, 360)):
        part = s1.at[pl.ds(0, rows)]
        pltpu.make_async_copy(part, part, send_sem.at[n]).wait()


def body(polar, azimuth, saturation, anisotropy, stiffness, coupling):
    vmem = pl.BlockSpec(memory_space=pltpu.VMEM)
    hbm = pl.BlockSpec(memory_space=pltpu.HBM)
    out = pltpu.VMEM((1, 3, 16, CELLS), f32)
    dma = pltpu.SemaphoreType.DMA
    block = pltpu.VMEM((SLAB * 12, 128), f32)
    row_block = pltpu.VMEM((1, 16, CELLS), f32)
    return pl.pallas_call(
        kernel,
        out_shape=(out, out),
        in_specs=[hbm] * 10,
        out_specs=(vmem, vmem),
        scratch_shapes=[
            row_block, row_block, row_block, row_block,
            pltpu.SMEM((1,), f32), pltpu.SMEM((LAYERS - 1,), f32),
            pltpu.VMEM((CELLS, PAD), bf16),
            pltpu.VMEM((CELLS, PAD), bf16),
            pltpu.VMEM((CELLS, PAD), bf16),
            pltpu.VMEM((CELLS, PAD), bf16),
            block, block, block, block, block, block, block, block,
            pltpu.VMEM((3 * 2 * 16 * 8, 128), f32),
            pltpu.VMEM((2, LAYERS, 4, 8, 128), f32),
            pltpu.VMEM((2, 8, 8, 128), f32),
            pltpu.VMEM((2, 2, 16, CELLS), f32),
            pltpu.VMEM((2, 16, 128), f32),
            pltpu.VMEM((2, 16, 128), f32),
            pltpu.VMEM((6, 16, CELLS), f32),
            dma((10,)), dma((4,)), dma((7,)), dma((4,)), dma((4,)), dma((2,)), dma((2,)),
        ],
        compiler_params=pltpu.CompilerParams(
            collective_id=0, has_side_effects=True, vmem_limit_bytes=60 * 1024 * 1024
        ),
        cost_estimate=pl.CostEstimate(flops=10**9, bytes_accessed=5 * 10**6, transcendentals=0),
        name="fields",
    )(polar, azimuth, saturation, anisotropy, stiffness, coupling, *transforms())


def solution(mesh):
    placed = (
        P("layer", "plane", None),
        P("layer", "plane", None),
        P("layer", "plane", None),
        P("layer", "plane", None),
        P("layer"),
        P(),
    )
    return jax.shard_map(
        body,
        mesh=mesh,
        in_specs=placed,
        out_specs=(P("layer", None, "plane", None), P("layer", None, "plane", None)),
        check_vma=False,
    )
```

```python
import functools
import math

import jax
import jax.numpy as jnp
import ml_dtypes
import numpy as np
from jax import lax
from jax.experimental import pallas as pl
from jax.experimental.pallas import tpu as pltpu
from jax.sharding import PartitionSpec as P

side_length = 512.0
spacing = 1.2
damping = 0.1
time_step = 0.1

CELLS = 512
PAD = 2 * CELLS
LAYERS = 16
RING = 16
SLAB = 32
MESH = pl.DeviceIdType.MESH
NEAR = [4, 12, 3, 13, 2, 14, 1, 15]
AWAY = [8, 7, 9, 6, 10, 5, 11, 4, 12, 3, 13, 2, 14, 1, 15]
FAR = [(a, b, dy) for a in range(2) for b in range(2) for dy in range(4)]
FAR.sort(key=lambda far: -((1 if far[1] else 2 * far[0]) + (0, 1, 2, 1)[far[2]]))
f32 = jnp.float32
bf16 = jnp.bfloat16


def halves(table):
    high = table.astype(ml_dtypes.bfloat16)
    low = (table - high.astype(np.float64)).astype(ml_dtypes.bfloat16)
    return high, low


@functools.lru_cache(None)
def transforms():
    column = np.arange(PAD)
    core, part = column // 512, column // 32 % 2
    wave = (column // 64 % 8 * 2 + column % 2) * SLAB + core * 16 + column // 2 % 16
    place = np.arange(CELLS)
    angle = (place[:, None] * wave[None, :] % PAD) * (2.0 * np.pi / PAD)
    along_y = np.where(part[None, :] == 0, np.cos(angle), np.sin(angle))
    alternating = np.where(place % 2 == 0, 1.0, -1.0)
    along_y[:, (wave == 0) & (part == 1)] = alternating[:, None]
    row = np.arange(CELLS)
    x = row // 256 * 256 + row % 16 * 16 + row // 128 % 2 * 8 + row // 64 % 2 * 4 + row // 16 % 4
    angle = (x[:, None] * np.arange(CELLS)[None, :] % PAD) * (2.0 * np.pi / PAD)
    sine = np.sin(angle)
    sine[:, 0] = np.where(x % 2 == 0, 1.0, -1.0)
    along_x = np.concatenate([np.cos(angle), sine], 1)
    return halves(along_y) + halves(along_x)


def polynomial(x, coefficients):
    total = jnp.full_like(x, coefficients[-1])
    for c in coefficients[-2::-1]:
        total = total * x + c
    return total


SIN = [(-1.0) ** n / math.factorial(2 * n + 1) for n in range(7)]
COS = [(-1.0) ** n / math.factorial(2 * n) for n in range(8)]
SINH = [1.0 / math.factorial(2 * n + 1) for n in range(11)]


def sin_cos(x):
    square = x * x
    return x * polynomial(square, SIN), polynomial(square, COS)


def unit_moment(polar, azimuth):
    sin_p, cos_p = sin_cos(polar)
    s, c = sin_cos(0.5 * azimuth)
    return sin_p * (1.0 - 2.0 * s * s), sin_p * (2.0 * s * c), cos_p


def product(left, high, low, transposed):
    left_high = left.astype(bf16)
    left_low = (left - left_high.astype(f32)).astype(bf16)
    rows = left.shape[0]
    dims = (((1,), (1 if transposed else 0,)), ((), ()))
    both = lax.dot_general(
        jnp.concatenate([left_high, left_low], 0), high, dims, preferred_element_type=f32
    )
    rest = lax.dot_general(left_high, low, dims, preferred_element_type=f32)
    return both[:rows] + both[rows:] + rest


def even_lanes():
    return lax.broadcasted_iota(jnp.int32, (8, 128), 1) % 2 == 0


def low_lanes(rows):
    return lax.broadcasted_iota(jnp.int32, (rows, 128), 1) < 64


def half_turn(x):
    return pltpu.roll(pltpu.roll(x, 64, 1), 4, 0)


def forward_y(m, saturation, wyh, wyl, s1):
    rows = [m[c][8 * h : 8 * h + 8] * saturation[8 * h : 8 * h + 8] for h in range(2) for c in range(3)]
    y = product(jnp.concatenate(rows, 0), wyh[...], wyl[...], False)
    even, low = even_lanes(), low_lanes(8)
    for c in range(3):
        for p in range(8):
            upper = y[8 * c : 8 * c + 8, 128 * p : 128 * p + 128]
            lower = y[24 + 8 * c : 32 + 8 * c, 128 * p : 128 * p + 128]
            first = jnp.where(even, upper, pltpu.roll(lower, 1, 1))
            second = jnp.where(even, pltpu.roll(upper, 127, 1), lower)
            for z, tile in ((p % 4 * 4, first), (p % 4 * 4 + 1, second)):
                turned = half_turn(tile)
                row = (p // 4 * 20 + z) * 12 + c * 4
                blocks = (jnp.where(low, tile, turned)[:4], jnp.where(low, turned, tile)[4:])
                for place, part in zip((row, row + 24), blocks):
                    s1[pl.ds(place, 4), :] = part
                    if p % 4 == 0:
                        s1[pl.ds(place + 192, 4), :] = part


def turn_in(k, r1, s2):
    for c in range(3):
        x = jnp.concatenate([r1[pl.ds(k * 192 + c * 4 + r, 16, stride=12), :] for r in range(4)], 0)
        block = jnp.concatenate([x, pltpu.roll(x, 64, 1)], 0).T
        for b in range(2):
            s2[pl.ds(k * 192 + 2 * c + b, 32, stride=6), :] = block[32 * b : 32 * b + 32]


def spectral_tables(fy, tb):
    sub = lax.broadcasted_iota(jnp.int32, (8, 128), 0)
    fx = sub % 4 * 128 + lax.broadcasted_iota(jnp.int32, (8, 128), 1)
    second = sub // 4 == 1
    sign = jnp.where(second, 1.0, -1.0)
    edge_x = fx == 0
    edge_y = jnp.full((8, 128), fy) == 0
    for v in range(2):
        sine_y = second if v == 0 else jnp.logical_not(second)
        high_x = jnp.logical_and(edge_x, second)
        high_y = jnp.logical_and(edge_y, sine_y)
        wave_x = jnp.where(high_x, CELLS, fx).astype(f32) * (math.pi / side_length)
        wave_y = jnp.where(high_y, CELLS, fy).astype(f32) * (math.pi / side_length)
        k = jnp.sqrt(wave_x * wave_x + wave_y * wave_y)
        nonzero = k > 0.0
        safe = jnp.where(nonzero, k, 1.0)
        inverse = 1.0 / safe
        half = 0.5 * safe
        ratio = polynomial(half * half, SINH)
        self_part = jnp.where(nonzero, jnp.exp(-half) * ratio, 1.0)
        mutual = jnp.where(nonzero, half * ratio * ratio, 0.0)
        weight = jnp.where(edge_x, 1.0, 2.0) * jnp.where(edge_y, 1.0, 2.0) * (1.0 / (PAD * PAD))
        ux, uy = wave_x * inverse, wave_y * inverse
        tb[v, 0] = jnp.exp(-spacing * k)
        tb[v, 1] = weight * (1.0 - self_part)
        tb[v, 2] = weight * mutual
        tb[v, 3] = weight * self_part
        tb[v, 4] = jnp.where(edge_x, 0.0, sign * ux)
        tb[v, 5] = jnp.where(edge_y, 0.0, sign * uy)
        tb[v, 6] = jnp.where(high_x, ux, 0.0)
        tb[v, 7] = jnp.where(high_y, uy, 0.0)


ORDER = [(0, 0), (1, 1), (0, 1), (1, 0)]
ORDER_X = [(1, 1), (0, 0), (1, 0), (0, 1)]


def tile_row(c, tg, cls, lb):
    return ((c * 2 + tg) * 16 + cls * 4 + lb) * 8


def transform_x(r2, wxh, wxl, zs):
    columns = []
    for x_lo in range(2):
        for h in range(2):
            parts = [r2[pl.ds(x_lo * 12 + h * 6 + q, 16, stride=24), :] for q in range(6)]
            columns.append(jnp.concatenate(parts, 0))
    z = product(jnp.concatenate(columns, 1), wxh[...], wxl[...], False)
    for c in range(3):
        for cls, (a, b) in enumerate(ORDER_X if c == 0 else ORDER):
            for tg in range(2):
                for lb in range(4):
                    row = (2 * c + b) * 16 + tg * 8
                    lane = a * 512 + lb * 128
                    zs[pl.ds(tile_row(c, tg, cls, lb), 8), :] = z[row : row + 8, lane : lane + 128]


def couple(zs, tb, ws):
    def at(c, t, v):
        return pl.ds(tile_row(c, t // 8, 2 * v, 0) + t % 8, 8, stride=8)

    for v in range(2):
        other = 1 - v
        decay, direct, mutual = tb[v, 0], tb[v, 1], tb[v, 2]
        ux, uy, lone_x, lone_y = tb[v, 4], tb[v, 5], tb[v, 6], tb[v, 7]
        if v == 1:
            uy = -uy
        carry = jnp.zeros((8, 128), f32)
        carry_lone = jnp.zeros((8, 128), f32)
        for t in range(LAYERS):
            r = ux * zs[at(0, t, other), :] + uy * zs[at(1, t, other), :]
            lone = lone_x * pltpu.roll(zs[at(0, t, v), :], 4, 0) + lone_y * zs[at(1, t, v), :]
            ws[v, t, 0] = r
            ws[v, t, 1] = lone
            ws[v, t, 2] = carry
            ws[v, t, 3] = carry_lone
            carry = decay * (carry + (zs[at(2, t, v), :] + r))
            carry_lone = decay * (carry_lone + lone)
    for v in range(2):
        decay, direct, mutual = tb[v, 0], tb[v, 1], tb[v, 2]
        carry = jnp.zeros((8, 128), f32)
        carry_lone = jnp.zeros((8, 128), f32)
        for t in range(LAYERS - 1, -1, -1):
            r, lone = ws[v, t, 0], ws[v, t, 1]
            below, below_lone = ws[v, t, 2], ws[v, t, 3]
            z = zs[at(2, t, v), :]
            ws[v, t, 0] = direct * r + mutual * (below + carry)
            ws[v, t, 1] = direct * lone + mutual * (below_lone + carry_lone)
            zs[at(2, t, v), :] = mutual * (below - carry) - tb[v, 3] * z
            carry = decay * (carry + (r - z))
            carry_lone = decay * (carry_lone + lone)
    for v in range(2):
        other = 1 - v
        ux, uy, lone_x, lone_y = tb[other, 4], tb[v, 5], tb[v, 6], tb[v, 7]
        if v == 1:
            uy = -uy
        for t in range(LAYERS):
            h, lone = ws[other, t, 0], ws[v, t, 1]
            zs[at(0, t, v), :] = -ux * h - pltpu.roll(lone_x * lone, 4, 0)
            zs[at(1, t, v), :] = uy * h - lone_y * lone


def return_x(zs, wxh, wxl, s3):
    rows = []
    for c in range(3):
        order = ORDER_X if c == 0 else ORDER
        for b in range(2):
            for tg in range(2):
                lanes = [
                    zs[pl.ds(tile_row(c, tg, order.index((a, b)), lb), 8), :] for a in range(2) for lb in range(4)
                ]
                rows.append(jnp.concatenate(lanes, 1))
    out = product(jnp.concatenate(rows, 0), wxh[...], wxl[...], True)
    for x_lo in range(2):
        for h in range(2):
            lane = (x_lo * 2 + h) * 128
            for q in range(6):
                s3[pl.ds(x_lo * 12 + h * 6 + q, 16, stride=24), :] = out[16 * q : 16 * q + 16, lane : lane + 128]


def turn_out(k, r3, s4):
    low = low_lanes(64)
    for c in range(3):
        parts = [r3[pl.ds(k * 192 + 2 * c + b, 32, stride=6), :] for b in range(2)]
        block = jnp.concatenate(parts + parts, 0).T
        block = jnp.where(low, block[:64], block[64:])
        for r in range(4):
            s4[pl.ds(k * 192 + c * 4 + r, 16, stride=12), :] = block[16 * r : 16 * r + 16]


def inverse_y(k, r4, wyh, wyl):
    even = even_lanes()
    kept = low_lanes(8) == (lax.broadcasted_iota(jnp.int32, (8, 128), 0) < 4)

    def tile(z, c):
        row = k * 192 + z * 12 + c * 4
        both = jnp.concatenate([r4[pl.ds(row, 4), :], r4[pl.ds(row + 24, 4), :]], 0)
        return jnp.where(kept, both, half_turn(both))

    upper, lower = [], []
    for c in range(3):
        up, low = [], []
        for p in range(4):
            first, second = tile(4 * p, c), tile(4 * p + 1, c)
            up.append(jnp.where(even, first, pltpu.roll(second, 1, 1)))
            low.append(jnp.where(even, pltpu.roll(first, 127, 1), second))
        upper.append(jnp.concatenate(up, 1))
        lower.append(jnp.concatenate(low, 1))
    columns = slice(512 * k, 512 * k + 512)
    return product(jnp.concatenate(upper + lower, 0), wyh[:, columns], wyl[:, columns], True)


def cross_product(a, b):
    return (a[1] * b[2] - a[2] * b[1], a[2] * b[0] - a[0] * b[2], a[0] * b[1] - a[1] * b[0])


def other_fields(m, first_row, last_row, lower_m, upper_m, stiffness, lower_link, upper_link, anisotropy):
    lane = lax.broadcasted_iota(jnp.int32, (16, 512), 1)
    fields = []
    for c in range(3):
        beside = jnp.concatenate([first_row[c], m[c][:15]], 0) + jnp.concatenate([m[c][1:], last_row[c]], 0)
        beside = beside + jnp.where(lane == 0, 0.0, pltpu.roll(m[c], 1, 1))
        beside = beside + jnp.where(lane == 511, 0.0, pltpu.roll(m[c], 511, 1))
        fields.append(stiffness * beside + lower_link * lower_m[c] + upper_link * upper_m[c])
    fields[2] = fields[2] + anisotropy * m[2]
    return fields


def step(m, field):
    first = cross_product(m, field)
    second = cross_product(m, first)
    scale = -time_step / (1.0 + damping * damping)
    stepped = [m[c] + scale * (first[c] + damping * second[c]) for c in range(3)]
    inverse = lax.rsqrt(stepped[0] * stepped[0] + stepped[1] * stepped[1] + stepped[2] * stepped[2])
    return [s * inverse for s in stepped]


def kernel(
    polar_any, azimuth_any, saturation_any, anisotropy_any, stiffness_any, coupling_any,
    wyh_any, wyl_any, wxh_any, wxl_any,
    field_out, moment_out,
    polar, azimuth, saturation, anisotropy, stiffness, coupling,
    wyh, wyl, wxh, wxl, s1, r1, s2, r2, s3, r3, s4, r4, zs, ws, tb, near, edge_out, edge_in, rest, relay,
    load_sem, send_sem, recv_sem, near_send, near_recv, edge_send, edge_recv, relay_sem,
):
    t = lax.axis_index("layer")
    p = lax.axis_index("plane")
    z = lax.rem(p, RING)
    x_lo = lax.div(p, RING)
    core = lax.rem(t, 2)
    y = lax.rem(lax.div(t, 2), 4)
    x_hi = lax.div(t, 8)
    source = t * 2 + x_lo
    owner = core * 16 + lax.div(t, 2) * 2 + x_lo

    def ring_device(away):
        there = lax.rem(z + away, RING)
        return there, (t, x_lo * RING + there)

    def slab_device(far, there_core):
        a, b, dy = far
        there_x = lax.rem(x_lo + b, 2)
        pair = lax.rem(x_hi + a, 2) * 4 + lax.rem(y + dy, 4)
        there_t = pair * 2 + there_core
        return there_t * 2 + there_x, there_core * 16 + pair * 2 + there_x, (there_t, there_x * RING + z)

    next_plane = (t, lax.rem(p + 1, 2 * RING))
    last_plane = (t, lax.rem(p + 2 * RING - 1, 2 * RING))
    next_layer = (lax.rem(t + 1, LAYERS), p)
    last_layer = (lax.rem(t + LAYERS - 1, LAYERS), p)

    barrier = pltpu.get_barrier_semaphore()

    def greet(there):
        pl.semaphore_signal(barrier, inc=1, device_id=there, device_id_type=MESH)

    for away in NEAR:
        greet(ring_device(away)[1])
    for far in FAR:
        greet(slab_device(far, 1 - core)[2])
        if any(far):
            greet(slab_device(far, core)[2])
    for there in (next_plane, last_plane):
        greet(there)

    loads = [
        pltpu.make_async_copy(src, dst, load_sem.at[i])
        for i, (src, dst) in enumerate([
            (polar_any, polar), (azimuth_any, azimuth), (saturation_any, saturation), (wyh_any, wyh), (wyl_any, wyl),
            (anisotropy_any, anisotropy), (stiffness_any, stiffness), (coupling_any, coupling),
            (wxh_any, wxh), (wxl_any, wxl),
        ])
    ]
    for load in loads:
        load.start()

    loads[0].wait()
    loads[1].wait()
    m = unit_moment(polar[0], azimuth[0])
    edge_out[...] = jnp.zeros((2, 16, 128), f32)
    for side, row in enumerate((0, 15)):
        for c in range(3):
            for lb in range(4):
                edge_out[side, c * 4 + lb : c * 4 + lb + 1, :] = m[c][row : row + 1, 128 * lb : 128 * lb + 128]
    for load in loads[2:5]:
        load.wait()
    forward_y(m, saturation[0], wyh, wyl, s1)

    pl.semaphore_wait(barrier, len(NEAR) + SLAB - 1 + 2)

    def remote(src, dst, sem, there):
        return pltpu.make_async_remote_copy(
            src_ref=src, dst_ref=dst, send_sem=sem[0], recv_sem=sem[1], device_id=there, device_id_type=MESH
        )

    def rows_of(ref, i):
        return ref.at[pl.ds(pl.multiple_of(i * 12, 4), 12)]

    def ring_send(src, dst, n, k, arrival):
        for away in AWAY:
            there, device = ring_device(away)
            sems = (send_sem.at[n], recv_sem.at[arrival])
            remote(rows_of(src, k * 16 + there), rows_of(dst, k * 16 + z), sems, device).start()
        pltpu.make_async_copy(rows_of(src, k * 16 + z), rows_of(dst, k * 16 + z), recv_sem.at[arrival]).start()

    def slab_send(k):
        sems = (send_sem.at[1], recv_sem.at[2])
        for far in FAR:
            _, there, device = slab_device(far, k)
            if any(far):
                remote(rows_of(s2, there), rows_of(r2, source), sems, device).start()
            else:

                @pl.when(core == k)
                def _():
                    pltpu.make_async_copy(rows_of(s2, owner), rows_of(r2, source), recv_sem.at[2]).start()

                @pl.when(core != k)
                def _():
                    remote(rows_of(s2, there), rows_of(r2, source), sems, device).start()

    def slab_return():
        sems = (send_sem.at[2], recv_sem.at[3 + core])
        for far in FAR:
            for there_core in (core, 1 - core):
                there, _, device = slab_device(far, there_core)
                if any(far) or there_core is not core:
                    remote(rows_of(s3, there), rows_of(r3, owner), sems, device).start()
        pltpu.make_async_copy(rows_of(s3, source), rows_of(r3, owner), recv_sem.at[3 + core]).start()

    def received(dst, n, rows=192):
        part = dst.at[pl.ds(0, rows)]
        pltpu.make_async_copy(part, part, recv_sem.at[n]).wait()

    before, from_before = ring_device(12)
    after, from_after = ring_device(4)

    def span(ref, first, count):
        return ref.at[pl.ds(pl.multiple_of(first * 12, 4), count * 12)]

    def send_far(k):
        up = span(s1, k * 20 + ring_device(5)[0], 4)
        down = span(s1, k * 20 + ring_device(9)[0], 3)
        remote(up, span(relay, k * 7, 4), (send_sem.at[0], relay_sem.at[2 * k]), from_after).start()
        remote(down, span(relay, k * 7 + 4, 3), (send_sem.at[0], relay_sem.at[2 * k + 1]), from_before).start()

    def send_near(k):
        for away in NEAR:
            there, device = ring_device(away)
            sems = (send_sem.at[0], recv_sem.at[k])
            remote(span(s1, k * 20 + there, 1), rows_of(r1, k * 16 + z), sems, device).start()
        pltpu.make_async_copy(span(s1, k * 20 + z, 1), rows_of(r1, k * 16 + z), recv_sem.at[k]).start()

    def pass_on(k):
        sems = (send_sem.at[4], recv_sem.at[k])
        for side, first, count, source_z, aways in (
            (0, k * 7, 4, before, (1, 2, 3, 4)), (1, k * 7 + 4, 3, after, (13, 14, 15)),
        ):
            arrived = span(relay, first, count)
            pltpu.make_async_copy(arrived, arrived, relay_sem.at[2 * k + side]).wait()
            order = sorted(range(count), key=lambda i: -min(aways[i], RING - aways[i]))
            for i in order:
                _, device = ring_device(aways[i])
                remote(span(relay, first + i, 1), rows_of(r1, k * 16 + source_z), sems, device).start()

    for k in range(2):
        send_far(k)
    for k in range(2):
        send_near(k)
    sides = []
    for i, (ref, side, there) in enumerate(
        [(polar, 0, next_layer), (azimuth, 0, next_layer), (polar, 1, last_layer), (azimuth, 1, last_layer)]
    ):
        sides.append(remote(ref.at[0], near.at[side, i % 2], (near_send.at[i], near_recv.at[i]), there))
    for side, there in ((0, last_plane), (1, next_plane)):
        sides.append(
            remote(edge_out.at[side], edge_in.at[1 - side], (edge_send.at[side], edge_recv.at[side]), there)
        )
    for copy in sides:
        copy.start()

    for load in loads[5:]:
        load.wait()
    spectral_tables(z * SLAB + owner, tb)
    for k in range(2):
        pass_on(k)
    for k in range(2):
        received(r1, k)
        turn_in(k, r1, s2)
        slab_send(k)
    for copy in sides:
        copy.wait_recv()
    lower_m = unit_moment(near[0, 0], near[0, 1])
    upper_m = unit_moment(near[1, 0], near[1, 1])
    lower_link = jnp.where(t > 0, coupling[jnp.maximum(t - 1, 0)], 0.0)
    upper_link = jnp.where(t < LAYERS - 1, coupling[jnp.minimum(t, LAYERS - 2)], 0.0)

    def edge_row(side, present):
        rows = []
        for c in range(3):
            lanes = [edge_in[side, c * 4 + lb : c * 4 + lb + 1, :] for lb in range(4)]
            rows.append(jnp.where(present, jnp.concatenate(lanes, 1), 0.0))
        return rows

    m = unit_moment(polar[0], azimuth[0])
    fields = other_fields(
        m, edge_row(0, p > 0), edge_row(1, p < 2 * RING - 1), lower_m, upper_m,
        stiffness[0], lower_link, upper_link, anisotropy[0],
    )
    for c in range(3):
        rest[c] = fields[c]
        rest[3 + c] = m[c]

    received(r2, 2, 384)
    transform_x(r2, wxh, wxl, zs)
    couple(zs, tb, ws)
    return_x(zs, wxh, wxl, s3)
    slab_return()
    for k in range(2):
        received(r3, 3 + k)
        turn_out(k, r3, s4)
        ring_send(s4, r4, 3, k, 5 + k)
    received(r4, 5)
    demag = inverse_y(0, r4, wyh, wyl)
    received(r4, 6)
    demag = demag + inverse_y(1, r4, wyh, wyl)
    m = [rest[3 + c] for c in range(3)]
    field = [
        jnp.concatenate([demag[8 * c : 8 * c + 8], demag[24 + 8 * c : 32 + 8 * c]], 0) + rest[c] for c in range(3)
    ]
    moment = step(m, field)
    for c in range(3):
        field_out[0, c] = field[c]
        moment_out[0, c] = moment[c]

    for copy in sides:
        copy.wait_send()
    for n, rows in ((0, 360), (1, 372), (2, 372), (3, 360), (4, 168)):
        part = s1.at[pl.ds(0, rows)]
        pltpu.make_async_copy(part, part, send_sem.at[n]).wait()


def body(polar, azimuth, saturation, anisotropy, stiffness, coupling):
    vmem = pl.BlockSpec(memory_space=pltpu.VMEM)
    hbm = pl.BlockSpec(memory_space=pltpu.HBM)
    out = pltpu.VMEM((1, 3, 16, CELLS), f32)
    dma = pltpu.SemaphoreType.DMA
    block = pltpu.VMEM((SLAB * 12, 128), f32)
    row_block = pltpu.VMEM((1, 16, CELLS), f32)
    return pl.pallas_call(
        kernel,
        out_shape=(out, out),
        in_specs=[hbm] * 10,
        out_specs=(vmem, vmem),
        scratch_shapes=[
            row_block, row_block, row_block, row_block,
            pltpu.SMEM((1,), f32), pltpu.SMEM((LAYERS - 1,), f32),
            pltpu.VMEM((CELLS, PAD), bf16),
            pltpu.VMEM((CELLS, PAD), bf16),
            pltpu.VMEM((CELLS, PAD), bf16),
            pltpu.VMEM((CELLS, PAD), bf16),
            pltpu.VMEM((2 * 20 * 12, 128), f32), block, block, block, block, block, block, block,
            pltpu.VMEM((3 * 2 * 16 * 8, 128), f32),
            pltpu.VMEM((2, LAYERS, 4, 8, 128), f32),
            pltpu.VMEM((2, 8, 8, 128), f32),
            pltpu.VMEM((2, 2, 16, CELLS), f32),
            pltpu.VMEM((2, 16, 128), f32),
            pltpu.VMEM((2, 16, 128), f32),
            pltpu.VMEM((6, 16, CELLS), f32),
            pltpu.VMEM((14 * 12, 128), f32),
            dma((10,)), dma((5,)), dma((7,)), dma((4,)), dma((4,)), dma((2,)), dma((2,)), dma((4,)),
        ],
        compiler_params=pltpu.CompilerParams(
            collective_id=0, has_side_effects=True, vmem_limit_bytes=60 * 1024 * 1024
        ),
        cost_estimate=pl.CostEstimate(flops=10**9, bytes_accessed=5 * 10**6, transcendentals=0),
        name="fields",
    )(polar, azimuth, saturation, anisotropy, stiffness, coupling, *transforms())


def solution(mesh):
    placed = (
        P("layer", "plane", None),
        P("layer", "plane", None),
        P("layer", "plane", None),
        P("layer", "plane", None),
        P("layer"),
        P(),
    )
    return jax.shard_map(
        body,
        mesh=mesh,
        in_specs=placed,
        out_specs=(P("layer", None, "plane", None), P("layer", None, "plane", None)),
        check_vma=False,
    )
```

```python
import functools
import math

import jax
import jax.numpy as jnp
import ml_dtypes
import numpy as np
from jax import lax
from jax.experimental import pallas as pl
from jax.experimental.pallas import tpu as pltpu
from jax.sharding import PartitionSpec as P

side_length = 512.0
spacing = 1.2
damping = 0.1
time_step = 0.1

CELLS = 512
PAD = 2 * CELLS
LAYERS = 16
RING = 16
SLAB = 32
MESH = pl.DeviceIdType.MESH
AWAY = [8, 7, 9, 6, 10, 5, 11, 4, 12, 3, 13, 2, 14, 1, 15]
FAR = [(a, b, dy) for a in range(2) for b in range(2) for dy in range(4)]
FAR.sort(key=lambda far: -((1 if far[1] else 2 * far[0]) + (0, 1, 2, 1)[far[2]]))
f32 = jnp.float32
bf16 = jnp.bfloat16


def halves(table):
    high = table.astype(ml_dtypes.bfloat16)
    low = (table - high.astype(np.float64)).astype(ml_dtypes.bfloat16)
    return high, low


@functools.lru_cache(None)
def transforms():
    column = np.arange(PAD)
    core, part = column // 512, column // 32 % 2
    wave = (column // 64 % 8 * 2 + column % 2) * SLAB + core * 16 + column // 2 % 16
    place = np.arange(CELLS)
    angle = (place[:, None] * wave[None, :] % PAD) * (2.0 * np.pi / PAD)
    along_y = np.where(part[None, :] == 0, np.cos(angle), np.sin(angle))
    alternating = np.where(place % 2 == 0, 1.0, -1.0)
    along_y[:, (wave == 0) & (part == 1)] = alternating[:, None]
    row = np.arange(CELLS)
    x = row // 256 * 256 + row % 16 * 16 + row // 128 % 2 * 8 + row // 64 % 2 * 4 + row // 16 % 4
    angle = (x[:, None] * np.arange(CELLS)[None, :] % PAD) * (2.0 * np.pi / PAD)
    sine = np.sin(angle)
    sine[:, 0] = np.where(x % 2 == 0, 1.0, -1.0)
    along_x = np.concatenate([np.cos(angle), sine], 1)
    return halves(along_y) + halves(along_x)


def polynomial(x, coefficients):
    total = jnp.full_like(x, coefficients[-1])
    for c in coefficients[-2::-1]:
        total = total * x + c
    return total


SIN = [(-1.0) ** n / math.factorial(2 * n + 1) for n in range(7)]
COS = [(-1.0) ** n / math.factorial(2 * n) for n in range(8)]
SINH = [1.0 / math.factorial(2 * n + 1) for n in range(11)]


def sin_cos(x):
    square = x * x
    return x * polynomial(square, SIN), polynomial(square, COS)


def unit_moment(polar, azimuth):
    sin_p, cos_p = sin_cos(polar)
    s, c = sin_cos(0.5 * azimuth)
    return sin_p * (1.0 - 2.0 * s * s), sin_p * (2.0 * s * c), cos_p


def product(left, high, low, transposed):
    left_high = left.astype(bf16)
    left_low = (left - left_high.astype(f32)).astype(bf16)
    rows = left.shape[0]
    dims = (((1,), (1 if transposed else 0,)), ((), ()))
    both = lax.dot_general(
        jnp.concatenate([left_high, left_low], 0), high, dims, preferred_element_type=f32
    )
    rest = lax.dot_general(left_high, low, dims, preferred_element_type=f32)
    return both[:rows] + both[rows:] + rest


def even_lanes():
    return lax.broadcasted_iota(jnp.int32, (8, 128), 1) % 2 == 0


def low_lanes(rows):
    return lax.broadcasted_iota(jnp.int32, (rows, 128), 1) < 64


def half_turn(x):
    return pltpu.roll(pltpu.roll(x, 64, 1), 4, 0)


def forward_y(m, saturation, wyh, wyl, s1):
    rows = [m[c][8 * h : 8 * h + 8] * saturation[8 * h : 8 * h + 8] for h in range(2) for c in range(3)]
    y = product(jnp.concatenate(rows, 0), wyh[...], wyl[...], False)
    even, low = even_lanes(), low_lanes(8)
    for c in range(3):
        for p in range(8):
            upper = y[8 * c : 8 * c + 8, 128 * p : 128 * p + 128]
            lower = y[24 + 8 * c : 32 + 8 * c, 128 * p : 128 * p + 128]
            first = jnp.where(even, upper, pltpu.roll(lower, 1, 1))
            second = jnp.where(even, pltpu.roll(upper, 127, 1), lower)
            for z, tile in ((p % 4 * 4, first), (p % 4 * 4 + 1, second)):
                turned = half_turn(tile)
                row = (p // 4 * 16 + z) * 12 + c * 4
                s1[pl.ds(row, 4), :] = jnp.where(low, tile, turned)[:4]
                s1[pl.ds(row + 24, 4), :] = jnp.where(low, turned, tile)[4:]


def turn_in(k, r1, s2):
    for c in range(3):
        x = jnp.concatenate([r1[pl.ds(k * 192 + c * 4 + r, 16, stride=12), :] for r in range(4)], 0)
        block = jnp.concatenate([x, pltpu.roll(x, 64, 1)], 0).T
        for b in range(2):
            s2[pl.ds(k * 192 + 2 * c + b, 32, stride=6), :] = block[32 * b : 32 * b + 32]


def spectral_tables(fy, tb):
    sub = lax.broadcasted_iota(jnp.int32, (8, 128), 0)
    fx = sub % 4 * 128 + lax.broadcasted_iota(jnp.int32, (8, 128), 1)
    second = sub // 4 == 1
    sign = jnp.where(second, 1.0, -1.0)
    edge_x = fx == 0
    edge_y = jnp.full((8, 128), fy) == 0
    for v in range(2):
        sine_y = second if v == 0 else jnp.logical_not(second)
        high_x = jnp.logical_and(edge_x, second)
        high_y = jnp.logical_and(edge_y, sine_y)
        wave_x = jnp.where(high_x, CELLS, fx).astype(f32) * (math.pi / side_length)
        wave_y = jnp.where(high_y, CELLS, fy).astype(f32) * (math.pi / side_length)
        k = jnp.sqrt(wave_x * wave_x + wave_y * wave_y)
        nonzero = k > 0.0
        safe = jnp.where(nonzero, k, 1.0)
        inverse = 1.0 / safe
        half = 0.5 * safe
        ratio = polynomial(half * half, SINH)
        self_part = jnp.where(nonzero, jnp.exp(-half) * ratio, 1.0)
        mutual = jnp.where(nonzero, half * ratio * ratio, 0.0)
        weight = jnp.where(edge_x, 1.0, 2.0) * jnp.where(edge_y, 1.0, 2.0) * (1.0 / (PAD * PAD))
        ux, uy = wave_x * inverse, wave_y * inverse
        tb[v, 0] = jnp.exp(-spacing * k)
        tb[v, 1] = weight * (1.0 - self_part)
        tb[v, 2] = weight * mutual
        tb[v, 3] = weight * self_part
        tb[v, 4] = jnp.where(edge_x, 0.0, sign * ux)
        tb[v, 5] = jnp.where(edge_y, 0.0, sign * uy)
        tb[v, 6] = jnp.where(high_x, ux, 0.0)
        tb[v, 7] = jnp.where(high_y, uy, 0.0)


ORDER = [(0, 0), (1, 1), (0, 1), (1, 0)]
ORDER_X = [(1, 1), (0, 0), (1, 0), (0, 1)]


def tile_row(c, tg, cls, lb):
    return ((c * 2 + tg) * 16 + cls * 4 + lb) * 8


def transform_x(r2, wxh, wxl, zs):
    columns = []
    for x_lo in range(2):
        for h in range(2):
            parts = [r2[pl.ds(x_lo * 12 + h * 6 + q, 16, stride=24), :] for q in range(6)]
            columns.append(jnp.concatenate(parts, 0))
    z = product(jnp.concatenate(columns, 1), wxh[...], wxl[...], False)
    for c in range(3):
        for cls, (a, b) in enumerate(ORDER_X if c == 0 else ORDER):
            for tg in range(2):
                for lb in range(4):
                    row = (2 * c + b) * 16 + tg * 8
                    lane = a * 512 + lb * 128
                    zs[pl.ds(tile_row(c, tg, cls, lb), 8), :] = z[row : row + 8, lane : lane + 128]


def couple(zs, tb, ws):
    def at(c, t, v):
        return pl.ds(tile_row(c, t // 8, 2 * v, 0) + t % 8, 8, stride=8)

    for v in range(2):
        other = 1 - v
        decay, direct, mutual = tb[v, 0], tb[v, 1], tb[v, 2]
        ux, uy, lone_x, lone_y = tb[v, 4], tb[v, 5], tb[v, 6], tb[v, 7]
        if v == 1:
            uy = -uy
        carry = jnp.zeros((8, 128), f32)
        carry_lone = jnp.zeros((8, 128), f32)
        for t in range(LAYERS):
            r = ux * zs[at(0, t, other), :] + uy * zs[at(1, t, other), :]
            lone = lone_x * pltpu.roll(zs[at(0, t, v), :], 4, 0) + lone_y * zs[at(1, t, v), :]
            ws[v, t, 0] = r
            ws[v, t, 1] = lone
            ws[v, t, 2] = carry
            ws[v, t, 3] = carry_lone
            carry = decay * (carry + (zs[at(2, t, v), :] + r))
            carry_lone = decay * (carry_lone + lone)
    for v in range(2):
        decay, direct, mutual = tb[v, 0], tb[v, 1], tb[v, 2]
        carry = jnp.zeros((8, 128), f32)
        carry_lone = jnp.zeros((8, 128), f32)
        for t in range(LAYERS - 1, -1, -1):
            r, lone = ws[v, t, 0], ws[v, t, 1]
            below, below_lone = ws[v, t, 2], ws[v, t, 3]
            z = zs[at(2, t, v), :]
            ws[v, t, 0] = direct * r + mutual * (below + carry)
            ws[v, t, 1] = direct * lone + mutual * (below_lone + carry_lone)
            zs[at(2, t, v), :] = mutual * (below - carry) - tb[v, 3] * z
            carry = decay * (carry + (r - z))
            carry_lone = decay * (carry_lone + lone)
    for v in range(2):
        other = 1 - v
        ux, uy, lone_x, lone_y = tb[other, 4], tb[v, 5], tb[v, 6], tb[v, 7]
        if v == 1:
            uy = -uy
        for t in range(LAYERS):
            h, lone = ws[other, t, 0], ws[v, t, 1]
            zs[at(0, t, v), :] = -ux * h - pltpu.roll(lone_x * lone, 4, 0)
            zs[at(1, t, v), :] = uy * h - lone_y * lone


def field_rows(zs):
    rows = []
    for c in range(3):
        order = ORDER_X if c == 0 else ORDER
        for b in range(2):
            for tg in range(2):
                lanes = [
                    zs[pl.ds(tile_row(c, tg, order.index((a, b)), lb), 8), :] for a in range(2) for lb in range(4)
                ]
                rows.append(jnp.concatenate(lanes, 1))
    return jnp.concatenate(rows, 0)


def return_x(x_lo, left, wxh, wxl, s3):
    wanted = pl.ds(pl.multiple_of(x_lo * 256, 256), 256)
    out = product(left, wxh[wanted, :], wxl[wanted, :], True)
    for h in range(2):
        for q in range(6):
            s3[pl.ds(x_lo * 12 + h * 6 + q, 16, stride=24), :] = out[16 * q : 16 * q + 16, h * 128 : h * 128 + 128]


def turn_out(k, r3, s4):
    low = low_lanes(64)
    for c in range(3):
        parts = [r3[pl.ds(k * 192 + 2 * c + b, 32, stride=6), :] for b in range(2)]
        block = jnp.concatenate(parts + parts, 0).T
        block = jnp.where(low, block[:64], block[64:])
        for r in range(4):
            s4[pl.ds(k * 192 + c * 4 + r, 16, stride=12), :] = block[16 * r : 16 * r + 16]


def inverse_y(k, r4, wyh, wyl):
    even = even_lanes()
    kept = low_lanes(8) == (lax.broadcasted_iota(jnp.int32, (8, 128), 0) < 4)

    def tile(z, c):
        row = k * 192 + z * 12 + c * 4
        both = jnp.concatenate([r4[pl.ds(row, 4), :], r4[pl.ds(row + 24, 4), :]], 0)
        return jnp.where(kept, both, half_turn(both))

    upper, lower = [], []
    for c in range(3):
        up, low = [], []
        for p in range(4):
            first, second = tile(4 * p, c), tile(4 * p + 1, c)
            up.append(jnp.where(even, first, pltpu.roll(second, 1, 1)))
            low.append(jnp.where(even, pltpu.roll(first, 127, 1), second))
        upper.append(jnp.concatenate(up, 1))
        lower.append(jnp.concatenate(low, 1))
    columns = slice(512 * k, 512 * k + 512)
    return product(jnp.concatenate(upper + lower, 0), wyh[:, columns], wyl[:, columns], True)


def cross_product(a, b):
    return (a[1] * b[2] - a[2] * b[1], a[2] * b[0] - a[0] * b[2], a[0] * b[1] - a[1] * b[0])


def other_fields(m, first_row, last_row, lower_m, upper_m, stiffness, lower_link, upper_link, anisotropy):
    lane = lax.broadcasted_iota(jnp.int32, (16, 512), 1)
    fields = []
    for c in range(3):
        beside = jnp.concatenate([first_row[c], m[c][:15]], 0) + jnp.concatenate([m[c][1:], last_row[c]], 0)
        beside = beside + jnp.where(lane == 0, 0.0, pltpu.roll(m[c], 1, 1))
        beside = beside + jnp.where(lane == 511, 0.0, pltpu.roll(m[c], 511, 1))
        fields.append(stiffness * beside + lower_link * lower_m[c] + upper_link * upper_m[c])
    fields[2] = fields[2] + anisotropy * m[2]
    return fields


def step(m, field):
    first = cross_product(m, field)
    second = cross_product(m, first)
    scale = -time_step / (1.0 + damping * damping)
    stepped = [m[c] + scale * (first[c] + damping * second[c]) for c in range(3)]
    inverse = lax.rsqrt(stepped[0] * stepped[0] + stepped[1] * stepped[1] + stepped[2] * stepped[2])
    return [s * inverse for s in stepped]


def kernel(
    polar_any, azimuth_any, saturation_any, anisotropy_any, stiffness_any, coupling_any,
    wyh_any, wyl_any, wxh_any, wxl_any,
    field_out, moment_out,
    polar, azimuth, saturation, anisotropy, stiffness, coupling,
    wyh, wyl, wxh, wxl, s1, r1, s2, r2, s3, r3, s4, r4, zs, ws, tb, near, edge_out, edge_in, rest,
    load_sem, send_sem, recv_sem, near_send, near_recv, edge_send, edge_recv,
):
    t = lax.axis_index("layer")
    p = lax.axis_index("plane")
    z = lax.rem(p, RING)
    x_lo = lax.div(p, RING)
    core = lax.rem(t, 2)
    y = lax.rem(lax.div(t, 2), 4)
    x_hi = lax.div(t, 8)
    source = t * 2 + x_lo
    owner = core * 16 + lax.div(t, 2) * 2 + x_lo

    def ring_device(away):
        there = lax.rem(z + away, RING)
        return there, (t, x_lo * RING + there)

    def slab_device(far, there_core):
        a, b, dy = far
        there_x = lax.rem(x_lo + b, 2)
        pair = lax.rem(x_hi + a, 2) * 4 + lax.rem(y + dy, 4)
        there_t = pair * 2 + there_core
        return there_t * 2 + there_x, there_core * 16 + pair * 2 + there_x, (there_t, there_x * RING + z)

    next_plane = (t, lax.rem(p + 1, 2 * RING))
    last_plane = (t, lax.rem(p + 2 * RING - 1, 2 * RING))
    next_layer = (lax.rem(t + 1, LAYERS), p)
    last_layer = (lax.rem(t + LAYERS - 1, LAYERS), p)

    barrier = pltpu.get_barrier_semaphore()

    def greet(there):
        pl.semaphore_signal(barrier, inc=1, device_id=there, device_id_type=MESH)

    for away in AWAY:
        greet(ring_device(away)[1])
    for far in FAR:
        greet(slab_device(far, 1 - core)[2])
        if any(far):
            greet(slab_device(far, core)[2])
    for there in (next_plane, last_plane):
        greet(there)

    loads = [
        pltpu.make_async_copy(src, dst, load_sem.at[i])
        for i, (src, dst) in enumerate([
            (polar_any, polar), (azimuth_any, azimuth), (saturation_any, saturation), (wyh_any, wyh), (wyl_any, wyl),
            (anisotropy_any, anisotropy), (stiffness_any, stiffness), (coupling_any, coupling),
            (wxh_any, wxh), (wxl_any, wxl),
        ])
    ]
    for load in loads:
        load.start()

    loads[0].wait()
    loads[1].wait()
    m = unit_moment(polar[0], azimuth[0])
    edge_out[...] = jnp.zeros((2, 16, 128), f32)
    for side, row in enumerate((0, 15)):
        for c in range(3):
            for lb in range(4):
                edge_out[side, c * 4 + lb : c * 4 + lb + 1, :] = m[c][row : row + 1, 128 * lb : 128 * lb + 128]
    for load in loads[2:5]:
        load.wait()
    forward_y(m, saturation[0], wyh, wyl, s1)

    pl.semaphore_wait(barrier, RING - 1 + SLAB - 1 + 2)

    def remote(src, dst, sem, there):
        return pltpu.make_async_remote_copy(
            src_ref=src, dst_ref=dst, send_sem=sem[0], recv_sem=sem[1], device_id=there, device_id_type=MESH
        )

    def rows_of(ref, i):
        return ref.at[pl.ds(pl.multiple_of(i * 12, 4), 12)]

    def ring_send(src, dst, n, k, arrival):
        for away in AWAY:
            there, device = ring_device(away)
            sems = (send_sem.at[n], recv_sem.at[arrival])
            remote(rows_of(src, k * 16 + there), rows_of(dst, k * 16 + z), sems, device).start()
        pltpu.make_async_copy(rows_of(src, k * 16 + z), rows_of(dst, k * 16 + z), recv_sem.at[arrival]).start()

    def slab_send(k):
        sems = (send_sem.at[1], recv_sem.at[2])
        for far in FAR:
            _, there, device = slab_device(far, k)
            if any(far):
                remote(rows_of(s2, there), rows_of(r2, source), sems, device).start()
            else:

                @pl.when(core == k)
                def _():
                    pltpu.make_async_copy(rows_of(s2, owner), rows_of(r2, source), recv_sem.at[2]).start()

                @pl.when(core != k)
                def _():
                    remote(rows_of(s2, there), rows_of(r2, source), sems, device).start()

    def slab_return(other):
        sems = (send_sem.at[2], recv_sem.at[3 + core])
        for far in [far for far in FAR if far[1] == other]:
            for there_core in (core, 1 - core):
                there, _, device = slab_device(far, there_core)
                if any(far) or there_core is not core:
                    remote(rows_of(s3, there), rows_of(r3, owner), sems, device).start()
        if not other:
            pltpu.make_async_copy(rows_of(s3, source), rows_of(r3, owner), recv_sem.at[3 + core]).start()

    def received(dst, n, rows=192):
        part = dst.at[pl.ds(0, rows)]
        pltpu.make_async_copy(part, part, recv_sem.at[n]).wait()

    for k in range(2):
        ring_send(s1, r1, 0, k, k)
    sides = []
    for i, (ref, side, there) in enumerate(
        [(polar, 0, next_layer), (azimuth, 0, next_layer), (polar, 1, last_layer), (azimuth, 1, last_layer)]
    ):
        sides.append(remote(ref.at[0], near.at[side, i % 2], (near_send.at[i], near_recv.at[i]), there))
    for side, there in ((0, last_plane), (1, next_plane)):
        sides.append(
            remote(edge_out.at[side], edge_in.at[1 - side], (edge_send.at[side], edge_recv.at[side]), there)
        )
    for copy in sides:
        copy.start()

    for load in loads[5:]:
        load.wait()
    spectral_tables(z * SLAB + owner, tb)
    for k in range(2):
        received(r1, k)
        turn_in(k, r1, s2)
        slab_send(k)
    for copy in sides:
        copy.wait_recv()
    lower_m = unit_moment(near[0, 0], near[0, 1])
    upper_m = unit_moment(near[1, 0], near[1, 1])
    lower_link = jnp.where(t > 0, coupling[jnp.maximum(t - 1, 0)], 0.0)
    upper_link = jnp.where(t < LAYERS - 1, coupling[jnp.minimum(t, LAYERS - 2)], 0.0)

    def edge_row(side, present):
        rows = []
        for c in range(3):
            lanes = [edge_in[side, c * 4 + lb : c * 4 + lb + 1, :] for lb in range(4)]
            rows.append(jnp.where(present, jnp.concatenate(lanes, 1), 0.0))
        return rows

    m = unit_moment(polar[0], azimuth[0])
    fields = other_fields(
        m, edge_row(0, p > 0), edge_row(1, p < 2 * RING - 1), lower_m, upper_m,
        stiffness[0], lower_link, upper_link, anisotropy[0],
    )
    for c in range(3):
        rest[c] = fields[c]
        rest[3 + c] = m[c]

    received(r2, 2, 384)
    transform_x(r2, wxh, wxl, zs)
    couple(zs, tb, ws)
    left = field_rows(zs)
    for other in range(2):
        return_x(lax.rem(x_lo + other, 2), left, wxh, wxl, s3)
        slab_return(other)
    for k in range(2):
        received(r3, 3 + k)
        turn_out(k, r3, s4)
        ring_send(s4, r4, 3, k, 5 + k)
    received(r4, 5)
    demag = inverse_y(0, r4, wyh, wyl)
    received(r4, 6)
    demag = demag + inverse_y(1, r4, wyh, wyl)
    m = [rest[3 + c] for c in range(3)]
    field = [
        jnp.concatenate([demag[8 * c : 8 * c + 8], demag[24 + 8 * c : 32 + 8 * c]], 0) + rest[c] for c in range(3)
    ]
    moment = step(m, field)
    for c in range(3):
        field_out[0, c] = field[c]
        moment_out[0, c] = moment[c]

    for copy in sides:
        copy.wait_send()
    for n, rows in ((0, 360), (1, 372), (2, 372), (3, 360)):
        part = s1.at[pl.ds(0, rows)]
        pltpu.make_async_copy(part, part, send_sem.at[n]).wait()


def body(polar, azimuth, saturation, anisotropy, stiffness, coupling):
    vmem = pl.BlockSpec(memory_space=pltpu.VMEM)
    hbm = pl.BlockSpec(memory_space=pltpu.HBM)
    out = pltpu.VMEM((1, 3, 16, CELLS), f32)
    dma = pltpu.SemaphoreType.DMA
    block = pltpu.VMEM((SLAB * 12, 128), f32)
    row_block = pltpu.VMEM((1, 16, CELLS), f32)
    return pl.pallas_call(
        kernel,
        out_shape=(out, out),
        in_specs=[hbm] * 10,
        out_specs=(vmem, vmem),
        scratch_shapes=[
            row_block, row_block, row_block, row_block,
            pltpu.SMEM((1,), f32), pltpu.SMEM((LAYERS - 1,), f32),
            pltpu.VMEM((CELLS, PAD), bf16),
            pltpu.VMEM((CELLS, PAD), bf16),
            pltpu.VMEM((CELLS, PAD), bf16),
            pltpu.VMEM((CELLS, PAD), bf16),
            block, block, block, block, block, block, block, block,
            pltpu.VMEM((3 * 2 * 16 * 8, 128), f32),
            pltpu.VMEM((2, LAYERS, 4, 8, 128), f32),
            pltpu.VMEM((2, 8, 8, 128), f32),
            pltpu.VMEM((2, 2, 16, CELLS), f32),
            pltpu.VMEM((2, 16, 128), f32),
            pltpu.VMEM((2, 16, 128), f32),
            pltpu.VMEM((6, 16, CELLS), f32),
            dma((10,)), dma((4,)), dma((7,)), dma((4,)), dma((4,)), dma((2,)), dma((2,)),
        ],
        compiler_params=pltpu.CompilerParams(
            collective_id=0, has_side_effects=True, vmem_limit_bytes=60 * 1024 * 1024
        ),
        cost_estimate=pl.CostEstimate(flops=10**9, bytes_accessed=5 * 10**6, transcendentals=0),
        name="fields",
    )(polar, azimuth, saturation, anisotropy, stiffness, coupling, *transforms())


def solution(mesh):
    placed = (
        P("layer", "plane", None),
        P("layer", "plane", None),
        P("layer", "plane", None),
        P("layer", "plane", None),
        P("layer"),
        P(),
    )
    return jax.shard_map(
        body,
        mesh=mesh,
        in_specs=placed,
        out_specs=(P("layer", None, "plane", None), P("layer", None, "plane", None)),
        check_vma=False,
    )
```

```python
import functools
import math

import jax
import jax.numpy as jnp
import ml_dtypes
import numpy as np
from jax import lax
from jax.experimental import pallas as pl
from jax.experimental.pallas import tpu as pltpu
from jax.sharding import PartitionSpec as P

side_length = 512.0
spacing = 1.2
damping = 0.1
time_step = 0.1

CELLS = 512
PAD = 2 * CELLS
LAYERS = 16
RING = 16
SLAB = 32
MESH = pl.DeviceIdType.MESH
AWAY = [8, 7, 9, 6, 10, 5, 11, 4, 12, 3, 13, 2, 14, 1, 15]
FAR = [(a, b, dy) for a in range(2) for b in range(2) for dy in range(4)]
FAR.sort(key=lambda far: -((1 if far[1] else 2 * far[0]) + (0, 1, 2, 1)[far[2]]))
f32 = jnp.float32
bf16 = jnp.bfloat16


def halves(table):
    high = table.astype(ml_dtypes.bfloat16)
    low = (table - high.astype(np.float64)).astype(ml_dtypes.bfloat16)
    return high, low


@functools.lru_cache(None)
def transforms():
    column = np.arange(PAD)
    core, part = column // 512, column // 32 % 2
    wave = (column // 64 % 8 * 2 + column % 2) * SLAB + core * 16 + column // 2 % 16
    place = np.arange(CELLS)
    angle = (place[:, None] * wave[None, :] % PAD) * (2.0 * np.pi / PAD)
    along_y = np.where(part[None, :] == 0, np.cos(angle), np.sin(angle))
    alternating = np.where(place % 2 == 0, 1.0, -1.0)
    along_y[:, (wave == 0) & (part == 1)] = alternating[:, None]
    row = np.arange(CELLS)
    x = row // 256 * 256 + row % 16 * 16 + row // 128 % 2 * 8 + row // 64 % 2 * 4 + row // 16 % 4
    angle = (x[:, None] * np.arange(CELLS)[None, :] % PAD) * (2.0 * np.pi / PAD)
    sine = np.sin(angle)
    sine[:, 0] = np.where(x % 2 == 0, 1.0, -1.0)
    along_x = np.concatenate([np.cos(angle), sine], 1)
    return halves(along_y) + halves(along_x)


def polynomial(x, coefficients):
    total = jnp.full_like(x, coefficients[-1])
    for c in coefficients[-2::-1]:
        total = total * x + c
    return total


SIN = [(-1.0) ** n / math.factorial(2 * n + 1) for n in range(7)]
COS = [(-1.0) ** n / math.factorial(2 * n) for n in range(8)]
SINH = [1.0 / math.factorial(2 * n + 1) for n in range(11)]


def sin_cos(x):
    square = x * x
    return x * polynomial(square, SIN), polynomial(square, COS)


def unit_moment(polar, azimuth):
    sin_p, cos_p = sin_cos(polar)
    s, c = sin_cos(0.5 * azimuth)
    return sin_p * (1.0 - 2.0 * s * s), sin_p * (2.0 * s * c), cos_p


def product(left, high, low, transposed):
    left_high = left.astype(bf16)
    left_low = (left - left_high.astype(f32)).astype(bf16)
    rows = left.shape[0]
    dims = (((1,), (1 if transposed else 0,)), ((), ()))
    both = lax.dot_general(
        jnp.concatenate([left_high, left_low], 0), high, dims, preferred_element_type=f32
    )
    rest = lax.dot_general(left_high, low, dims, preferred_element_type=f32)
    return both[:rows] + both[rows:] + rest


def even_lanes():
    return lax.broadcasted_iota(jnp.int32, (8, 128), 1) % 2 == 0


def low_lanes(rows):
    return lax.broadcasted_iota(jnp.int32, (rows, 128), 1) < 64


def half_turn(x):
    return pltpu.roll(pltpu.roll(x, 64, 1), 4, 0)


def forward_y(m, saturation, wyh, wyl, s1):
    rows = [m[c][8 * h : 8 * h + 8] * saturation[8 * h : 8 * h + 8] for h in range(2) for c in range(3)]
    y = product(jnp.concatenate(rows, 0), wyh[...], wyl[...], False)
    even, low = even_lanes(), low_lanes(8)
    for c in range(3):
        for p in range(8):
            upper = y[8 * c : 8 * c + 8, 128 * p : 128 * p + 128]
            lower = y[24 + 8 * c : 32 + 8 * c, 128 * p : 128 * p + 128]
            first = jnp.where(even, upper, pltpu.roll(lower, 1, 1))
            second = jnp.where(even, pltpu.roll(upper, 127, 1), lower)
            for z, tile in ((p % 4 * 4, first), (p % 4 * 4 + 1, second)):
                turned = half_turn(tile)
                row = (p // 4 * 16 + z) * 12 + c * 4
                s1[pl.ds(row, 4), :] = jnp.where(low, tile, turned)[:4]
                s1[pl.ds(row + 24, 4), :] = jnp.where(low, turned, tile)[4:]


def turn_in(k, r1, s2):
    for c in range(3):
        x = jnp.concatenate([r1[pl.ds(k * 192 + c * 4 + r, 16, stride=12), :] for r in range(4)], 0)
        block = jnp.concatenate([x, pltpu.roll(x, 64, 1)], 0).T
        for b in range(2):
            s2[pl.ds(k * 192 + 2 * c + b, 32, stride=6), :] = block[32 * b : 32 * b + 32]


def spectral_tables(fy, tb):
    sub = lax.broadcasted_iota(jnp.int32, (8, 128), 0)
    fx = sub % 4 * 128 + lax.broadcasted_iota(jnp.int32, (8, 128), 1)
    second = sub // 4 == 1
    sign = jnp.where(second, 1.0, -1.0)
    edge_x = fx == 0
    edge_y = jnp.full((8, 128), fy) == 0
    for v in range(2):
        sine_y = second if v == 0 else jnp.logical_not(second)
        high_x = jnp.logical_and(edge_x, second)
        high_y = jnp.logical_and(edge_y, sine_y)
        wave_x = jnp.where(high_x, CELLS, fx).astype(f32) * (math.pi / side_length)
        wave_y = jnp.where(high_y, CELLS, fy).astype(f32) * (math.pi / side_length)
        k = jnp.sqrt(wave_x * wave_x + wave_y * wave_y)
        nonzero = k > 0.0
        safe = jnp.where(nonzero, k, 1.0)
        inverse = 1.0 / safe
        half = 0.5 * safe
        ratio = polynomial(half * half, SINH)
        self_part = jnp.where(nonzero, jnp.exp(-half) * ratio, 1.0)
        mutual = jnp.where(nonzero, half * ratio * ratio, 0.0)
        weight = jnp.where(edge_x, 1.0, 2.0) * jnp.where(edge_y, 1.0, 2.0) * (1.0 / (PAD * PAD))
        ux, uy = wave_x * inverse, wave_y * inverse
        tb[v, 0] = jnp.exp(-spacing * k)
        tb[v, 1] = weight * (1.0 - self_part)
        tb[v, 2] = weight * mutual
        tb[v, 3] = weight * self_part
        tb[v, 4] = jnp.where(edge_x, 0.0, sign * ux)
        tb[v, 5] = jnp.where(edge_y, 0.0, sign * uy)
        tb[v, 6] = jnp.where(high_x, ux, 0.0)
        tb[v, 7] = jnp.where(high_y, uy, 0.0)


ORDER = [(0, 0), (1, 1), (0, 1), (1, 0)]
ORDER_X = [(1, 1), (0, 0), (1, 0), (0, 1)]


def tile_row(c, tg, cls, lb):
    return ((c * 2 + tg) * 16 + cls * 4 + lb) * 8


def transform_x(r2, wxh, wxl, zs):
    columns = []
    for x_lo in range(2):
        for h in range(2):
            parts = [r2[pl.ds(x_lo * 12 + h * 6 + q, 16, stride=24), :] for q in range(6)]
            columns.append(jnp.concatenate(parts, 0))
    z = product(jnp.concatenate(columns, 1), wxh[...], wxl[...], False)
    for c in range(3):
        for cls, (a, b) in enumerate(ORDER_X if c == 0 else ORDER):
            for tg in range(2):
                for lb in range(4):
                    row = (2 * c + b) * 16 + tg * 8
                    lane = a * 512 + lb * 128
                    zs[pl.ds(tile_row(c, tg, cls, lb), 8), :] = z[row : row + 8, lane : lane + 128]


def couple(zs, tb, ws):
    def at(c, t, v):
        return pl.ds(tile_row(c, t // 8, 2 * v, 0) + t % 8, 8, stride=8)

    for v in range(2):
        other = 1 - v
        decay, direct, mutual = tb[v, 0], tb[v, 1], tb[v, 2]
        ux, uy, lone_x, lone_y = tb[v, 4], tb[v, 5], tb[v, 6], tb[v, 7]
        if v == 1:
            uy = -uy
        carry = jnp.zeros((8, 128), f32)
        carry_lone = jnp.zeros((8, 128), f32)
        for t in range(LAYERS):
            r = ux * zs[at(0, t, other), :] + uy * zs[at(1, t, other), :]
            lone = lone_x * pltpu.roll(zs[at(0, t, v), :], 4, 0) + lone_y * zs[at(1, t, v), :]
            ws[v, t, 0] = r
            ws[v, t, 1] = lone
            ws[v, t, 2] = carry
            ws[v, t, 3] = carry_lone
            carry = decay * (carry + (zs[at(2, t, v), :] + r))
            carry_lone = decay * (carry_lone + lone)
    for v in range(2):
        decay, direct, mutual = tb[v, 0], tb[v, 1], tb[v, 2]
        carry = jnp.zeros((8, 128), f32)
        carry_lone = jnp.zeros((8, 128), f32)
        for t in range(LAYERS - 1, -1, -1):
            r, lone = ws[v, t, 0], ws[v, t, 1]
            below, below_lone = ws[v, t, 2], ws[v, t, 3]
            z = zs[at(2, t, v), :]
            ws[v, t, 0] = direct * r + mutual * (below + carry)
            ws[v, t, 1] = direct * lone + mutual * (below_lone + carry_lone)
            zs[at(2, t, v), :] = mutual * (below - carry) - tb[v, 3] * z
            carry = decay * (carry + (r - z))
            carry_lone = decay * (carry_lone + lone)
    for v in range(2):
        other = 1 - v
        ux, uy, lone_x, lone_y = tb[other, 4], tb[v, 5], tb[v, 6], tb[v, 7]
        if v == 1:
            uy = -uy
        for t in range(LAYERS):
            h, lone = ws[other, t, 0], ws[v, t, 1]
            zs[at(0, t, v), :] = -ux * h - pltpu.roll(lone_x * lone, 4, 0)
            zs[at(1, t, v), :] = uy * h - lone_y * lone


def return_x(zs, wxh, wxl, s3):
    rows = []
    for c in range(3):
        order = ORDER_X if c == 0 else ORDER
        for b in range(2):
            for tg in range(2):
                lanes = [
                    zs[pl.ds(tile_row(c, tg, order.index((a, b)), lb), 8), :] for a in range(2) for lb in range(4)
                ]
                rows.append(jnp.concatenate(lanes, 1))
    out = product(jnp.concatenate(rows, 0), wxh[...], wxl[...], True)
    for x_lo in range(2):
        for h in range(2):
            lane = (x_lo * 2 + h) * 128
            for q in range(6):
                s3[pl.ds(x_lo * 12 + h * 6 + q, 16, stride=24), :] = out[16 * q : 16 * q + 16, lane : lane + 128]


def turn_out(k, r3, s4):
    low = low_lanes(64)
    for c in range(3):
        parts = [r3[pl.ds(k * 192 + 2 * c + b, 32, stride=6), :] for b in range(2)]
        block = jnp.concatenate(parts + parts, 0).T
        block = jnp.where(low, block[:64], block[64:])
        for r in range(4):
            s4[pl.ds(k * 192 + c * 4 + r, 16, stride=12), :] = block[16 * r : 16 * r + 16]


def inverse_y(k, r4, wyh, wyl):
    even = even_lanes()
    kept = low_lanes(8) == (lax.broadcasted_iota(jnp.int32, (8, 128), 0) < 4)

    def tile(z, c):
        row = k * 192 + z * 12 + c * 4
        both = jnp.concatenate([r4[pl.ds(row, 4), :], r4[pl.ds(row + 24, 4), :]], 0)
        return jnp.where(kept, both, half_turn(both))

    upper, lower = [], []
    for c in range(3):
        up, low = [], []
        for p in range(4):
            first, second = tile(4 * p, c), tile(4 * p + 1, c)
            up.append(jnp.where(even, first, pltpu.roll(second, 1, 1)))
            low.append(jnp.where(even, pltpu.roll(first, 127, 1), second))
        upper.append(jnp.concatenate(up, 1))
        lower.append(jnp.concatenate(low, 1))
    columns = slice(512 * k, 512 * k + 512)
    return product(jnp.concatenate(upper + lower, 0), wyh[:, columns], wyl[:, columns], True)


def cross_product(a, b):
    return (a[1] * b[2] - a[2] * b[1], a[2] * b[0] - a[0] * b[2], a[0] * b[1] - a[1] * b[0])


def other_fields(m, first_row, last_row, lower_m, upper_m, stiffness, lower_link, upper_link, anisotropy):
    lane = lax.broadcasted_iota(jnp.int32, (16, 512), 1)
    fields = []
    for c in range(3):
        beside = jnp.concatenate([first_row[c], m[c][:15]], 0) + jnp.concatenate([m[c][1:], last_row[c]], 0)
        beside = beside + jnp.where(lane == 0, 0.0, pltpu.roll(m[c], 1, 1))
        beside = beside + jnp.where(lane == 511, 0.0, pltpu.roll(m[c], 511, 1))
        fields.append(stiffness * beside + lower_link * lower_m[c] + upper_link * upper_m[c])
    fields[2] = fields[2] + anisotropy * m[2]
    return fields


def step(m, field):
    first = cross_product(m, field)
    second = cross_product(m, first)
    scale = -time_step / (1.0 + damping * damping)
    stepped = [m[c] + scale * (first[c] + damping * second[c]) for c in range(3)]
    inverse = lax.rsqrt(stepped[0] * stepped[0] + stepped[1] * stepped[1] + stepped[2] * stepped[2])
    return [s * inverse for s in stepped]


def kernel(
    polar_any, azimuth_any, saturation_any, anisotropy_any, stiffness_any, coupling_any,
    wyh_any, wyl_any, wxh_any, wxl_any,
    field_out, moment_out,
    polar, azimuth, saturation, anisotropy, stiffness, coupling,
    wyh, wyl, wxh, wxl, s1, r1, s2, r2, s3, r3, s4, r4, zs, ws, tb, near, edge_out, edge_in, rest,
    load_sem, send_sem, recv_sem, near_send, near_recv, edge_send, edge_recv,
):
    t = lax.axis_index("layer")
    p = lax.axis_index("plane")
    z = lax.rem(p, RING)
    x_lo = lax.div(p, RING)
    core = lax.rem(t, 2)
    y = lax.rem(lax.div(t, 2), 4)
    x_hi = lax.div(t, 8)
    source = t * 2 + x_lo
    owner = core * 16 + lax.div(t, 2) * 2 + x_lo

    def ring_device(away):
        there = lax.rem(z + away, RING)
        return there, (t, x_lo * RING + there)

    def slab_device(far, there_core):
        a, b, dy = far
        there_x = lax.rem(x_lo + b, 2)
        pair = lax.rem(x_hi + a, 2) * 4 + lax.rem(y + dy, 4)
        there_t = pair * 2 + there_core
        return there_t * 2 + there_x, there_core * 16 + pair * 2 + there_x, (there_t, there_x * RING + z)

    next_plane = (t, lax.rem(p + 1, 2 * RING))
    last_plane = (t, lax.rem(p + 2 * RING - 1, 2 * RING))
    next_layer = (lax.rem(t + 1, LAYERS), p)
    last_layer = (lax.rem(t + LAYERS - 1, LAYERS), p)

    barrier = pltpu.get_barrier_semaphore()

    def greet(there):
        pl.semaphore_signal(barrier, inc=1, device_id=there, device_id_type=MESH)

    for away in AWAY:
        greet(ring_device(away)[1])
    for far in FAR:
        greet(slab_device(far, 1 - core)[2])
        if any(far):
            greet(slab_device(far, core)[2])
    for there in (next_plane, last_plane):
        greet(there)

    loads = [
        pltpu.make_async_copy(src, dst, load_sem.at[i])
        for i, (src, dst) in enumerate([
            (polar_any, polar), (azimuth_any, azimuth), (saturation_any, saturation), (wyh_any, wyh), (wyl_any, wyl),
            (anisotropy_any, anisotropy), (stiffness_any, stiffness), (coupling_any, coupling),
            (wxh_any, wxh), (wxl_any, wxl),
        ])
    ]
    for load in loads:
        load.start()

    loads[0].wait()
    loads[1].wait()
    m = unit_moment(polar[0], azimuth[0])
    edge_out[...] = jnp.zeros((2, 16, 128), f32)
    for side, row in enumerate((0, 15)):
        for c in range(3):
            for lb in range(4):
                edge_out[side, c * 4 + lb : c * 4 + lb + 1, :] = m[c][row : row + 1, 128 * lb : 128 * lb + 128]
    for load in loads[2:5]:
        load.wait()
    forward_y(m, saturation[0], wyh, wyl, s1)

    pl.semaphore_wait(barrier, RING - 1 + SLAB - 1 + 2)

    def remote(src, dst, sem, there):
        return pltpu.make_async_remote_copy(
            src_ref=src, dst_ref=dst, send_sem=sem[0], recv_sem=sem[1], device_id=there, device_id_type=MESH
        )

    def rows_of(ref, i):
        return ref.at[pl.ds(pl.multiple_of(i * 12, 4), 12)]

    def ring_send(src, dst, n, k, arrival):
        for away in AWAY:
            there, device = ring_device(away)
            sems = (send_sem.at[n], recv_sem.at[arrival])
            remote(rows_of(src, k * 16 + there), rows_of(dst, k * 16 + z), sems, device).start()
        pltpu.make_async_copy(rows_of(src, k * 16 + z), rows_of(dst, k * 16 + z), recv_sem.at[arrival]).start()

    def slab_send(k):
        sems = (send_sem.at[1], recv_sem.at[2])
        for far in FAR:
            _, there, device = slab_device(far, k)
            if any(far):
                remote(rows_of(s2, there), rows_of(r2, source), sems, device).start()
            else:

                @pl.when(core == k)
                def _():
                    pltpu.make_async_copy(rows_of(s2, owner), rows_of(r2, source), recv_sem.at[2]).start()

                @pl.when(core != k)
                def _():
                    remote(rows_of(s2, there), rows_of(r2, source), sems, device).start()

    def slab_return():
        sems = (send_sem.at[2], recv_sem.at[3 + core])
        for far in FAR:
            for there_core in (1 - core, core):
                there, _, device = slab_device(far, there_core)
                if any(far) or there_core is not core:
                    remote(rows_of(s3, there), rows_of(r3, owner), sems, device).start()
        pltpu.make_async_copy(rows_of(s3, source), rows_of(r3, owner), recv_sem.at[3 + core]).start()

    def received(dst, n, rows=192):
        part = dst.at[pl.ds(0, rows)]
        pltpu.make_async_copy(part, part, recv_sem.at[n]).wait()

    for k in range(2):
        ring_send(s1, r1, 0, k, k)
    sides = []
    for i, (ref, side, there) in enumerate(
        [(polar, 0, next_layer), (azimuth, 0, next_layer), (polar, 1, last_layer), (azimuth, 1, last_layer)]
    ):
        sides.append(remote(ref.at[0], near.at[side, i % 2], (near_send.at[i], near_recv.at[i]), there))
    for side, there in ((0, last_plane), (1, next_plane)):
        sides.append(
            remote(edge_out.at[side], edge_in.at[1 - side], (edge_send.at[side], edge_recv.at[side]), there)
        )
    for copy in sides:
        copy.start()

    for load in loads[5:]:
        load.wait()
    spectral_tables(z * SLAB + owner, tb)
    for k in range(2):
        received(r1, k)
        turn_in(k, r1, s2)
        slab_send(k)
    for copy in sides:
        copy.wait_recv()
    lower_m = unit_moment(near[0, 0], near[0, 1])
    upper_m = unit_moment(near[1, 0], near[1, 1])
    lower_link = jnp.where(t > 0, coupling[jnp.maximum(t - 1, 0)], 0.0)
    upper_link = jnp.where(t < LAYERS - 1, coupling[jnp.minimum(t, LAYERS - 2)], 0.0)

    def edge_row(side, present):
        rows = []
        for c in range(3):
            lanes = [edge_in[side, c * 4 + lb : c * 4 + lb + 1, :] for lb in range(4)]
            rows.append(jnp.where(present, jnp.concatenate(lanes, 1), 0.0))
        return rows

    m = unit_moment(polar[0], azimuth[0])
    fields = other_fields(
        m, edge_row(0, p > 0), edge_row(1, p < 2 * RING - 1), lower_m, upper_m,
        stiffness[0], lower_link, upper_link, anisotropy[0],
    )
    for c in range(3):
        rest[c] = fields[c]
        rest[3 + c] = m[c]

    received(r2, 2, 384)
    transform_x(r2, wxh, wxl, zs)
    couple(zs, tb, ws)
    return_x(zs, wxh, wxl, s3)
    slab_return()
    for k in range(2):
        received(r3, 3 + k)
        turn_out(k, r3, s4)
        ring_send(s4, r4, 3, k, 5 + k)
    received(r4, 5)
    demag = inverse_y(0, r4, wyh, wyl)
    received(r4, 6)
    demag = demag + inverse_y(1, r4, wyh, wyl)
    m = [rest[3 + c] for c in range(3)]
    field = [
        jnp.concatenate([demag[8 * c : 8 * c + 8], demag[24 + 8 * c : 32 + 8 * c]], 0) + rest[c] for c in range(3)
    ]
    moment = step(m, field)
    for c in range(3):
        field_out[0, c] = field[c]
        moment_out[0, c] = moment[c]

    for copy in sides:
        copy.wait_send()
    for n, rows in ((0, 360), (1, 372), (2, 372), (3, 360)):
        part = s1.at[pl.ds(0, rows)]
        pltpu.make_async_copy(part, part, send_sem.at[n]).wait()


def body(polar, azimuth, saturation, anisotropy, stiffness, coupling):
    vmem = pl.BlockSpec(memory_space=pltpu.VMEM)
    hbm = pl.BlockSpec(memory_space=pltpu.HBM)
    out = pltpu.VMEM((1, 3, 16, CELLS), f32)
    dma = pltpu.SemaphoreType.DMA
    block = pltpu.VMEM((SLAB * 12, 128), f32)
    row_block = pltpu.VMEM((1, 16, CELLS), f32)
    return pl.pallas_call(
        kernel,
        out_shape=(out, out),
        in_specs=[hbm] * 10,
        out_specs=(vmem, vmem),
        scratch_shapes=[
            row_block, row_block, row_block, row_block,
            pltpu.SMEM((1,), f32), pltpu.SMEM((LAYERS - 1,), f32),
            pltpu.VMEM((CELLS, PAD), bf16),
            pltpu.VMEM((CELLS, PAD), bf16),
            pltpu.VMEM((CELLS, PAD), bf16),
            pltpu.VMEM((CELLS, PAD), bf16),
            block, block, block, block, block, block, block, block,
            pltpu.VMEM((3 * 2 * 16 * 8, 128), f32),
            pltpu.VMEM((2, LAYERS, 4, 8, 128), f32),
            pltpu.VMEM((2, 8, 8, 128), f32),
            pltpu.VMEM((2, 2, 16, CELLS), f32),
            pltpu.VMEM((2, 16, 128), f32),
            pltpu.VMEM((2, 16, 128), f32),
            pltpu.VMEM((6, 16, CELLS), f32),
            dma((10,)), dma((4,)), dma((7,)), dma((4,)), dma((4,)), dma((2,)), dma((2,)),
        ],
        compiler_params=pltpu.CompilerParams(
            collective_id=0, has_side_effects=True, vmem_limit_bytes=60 * 1024 * 1024
        ),
        cost_estimate=pl.CostEstimate(flops=10**9, bytes_accessed=5 * 10**6, transcendentals=0),
        name="fields",
    )(polar, azimuth, saturation, anisotropy, stiffness, coupling, *transforms())


def solution(mesh):
    placed = (
        P("layer", "plane", None),
        P("layer", "plane", None),
        P("layer", "plane", None),
        P("layer", "plane", None),
        P("layer"),
        P(),
    )
    return jax.shard_map(
        body,
        mesh=mesh,
        in_specs=placed,
        out_specs=(P("layer", None, "plane", None), P("layer", None, "plane", None)),
        check_vma=False,
    )
```

```python
import functools
import math

import jax
import jax.numpy as jnp
import ml_dtypes
import numpy as np
from jax import lax
from jax.experimental import pallas as pl
from jax.experimental.pallas import tpu as pltpu
from jax.sharding import PartitionSpec as P

side_length = 512.0
spacing = 1.2
damping = 0.1
time_step = 0.1

CELLS = 512
PAD = 2 * CELLS
LAYERS = 16
RING = 16
SLAB = 32
MESH = pl.DeviceIdType.MESH
AWAY = [8, 7, 9, 6, 10, 5, 11, 4, 12, 3, 13, 2, 14, 1, 15]
FAR = [(a, b, dy) for a in range(2) for b in range(2) for dy in range(4)]
FAR.sort(key=lambda far: -((1 if far[1] else 2 * far[0]) + (0, 1, 2, 1)[far[2]]))
f32 = jnp.float32
bf16 = jnp.bfloat16


def halves(table):
    high = table.astype(ml_dtypes.bfloat16)
    low = (table - high.astype(np.float64)).astype(ml_dtypes.bfloat16)
    return high, low


@functools.lru_cache(None)
def transforms():
    column = np.arange(PAD)
    core, part = column // 512, column // 32 % 2
    wave = (column // 64 % 8 * 2 + column % 2) * SLAB + core * 16 + column // 2 % 16
    place = np.arange(CELLS)
    angle = (place[:, None] * wave[None, :] % PAD) * (2.0 * np.pi / PAD)
    along_y = np.where(part[None, :] == 0, np.cos(angle), np.sin(angle))
    alternating = np.where(place % 2 == 0, 1.0, -1.0)
    along_y[:, (wave == 0) & (part == 1)] = alternating[:, None]
    row = np.arange(CELLS)
    x = row // 256 * 256 + row % 16 * 16 + row // 128 % 2 * 8 + row // 64 % 2 * 4 + row // 16 % 4
    angle = (x[:, None] * np.arange(CELLS)[None, :] % PAD) * (2.0 * np.pi / PAD)
    sine = np.sin(angle)
    sine[:, 0] = np.where(x % 2 == 0, 1.0, -1.0)
    along_x = np.concatenate([np.cos(angle), sine], 1)
    return sum((halves(table) for table in (along_y, along_x, along_x.T, along_y.T)), ())


def polynomial(x, coefficients):
    total = jnp.full_like(x, coefficients[-1])
    for c in coefficients[-2::-1]:
        total = total * x + c
    return total


SIN = [(-1.0) ** n / math.factorial(2 * n + 1) for n in range(7)]
COS = [(-1.0) ** n / math.factorial(2 * n) for n in range(8)]
SINH = [1.0 / math.factorial(2 * n + 1) for n in range(11)]


def sin_cos(x):
    square = x * x
    return x * polynomial(square, SIN), polynomial(square, COS)


def unit_moment(polar, azimuth):
    sin_p, cos_p = sin_cos(polar)
    s, c = sin_cos(0.5 * azimuth)
    return sin_p * (1.0 - 2.0 * s * s), sin_p * (2.0 * s * c), cos_p


def product(left, high, low):
    left_high = left.astype(bf16)
    left_low = (left - left_high.astype(f32)).astype(bf16)
    rows = left.shape[0]
    dims = (((1,), (0,)), ((), ()))
    both = lax.dot_general(
        jnp.concatenate([left_high, left_low], 0), high, dims, preferred_element_type=f32
    )
    rest = lax.dot_general(left_high, low, dims, preferred_element_type=f32)
    return both[:rows] + both[rows:] + rest


def even_lanes():
    return lax.broadcasted_iota(jnp.int32, (8, 128), 1) % 2 == 0


def low_lanes(rows):
    return lax.broadcasted_iota(jnp.int32, (rows, 128), 1) < 64


def half_turn(x):
    return pltpu.roll(pltpu.roll(x, 64, 1), 4, 0)


def forward_y(m, saturation, wyh, wyl, s1):
    rows = [m[c][8 * h : 8 * h + 8] * saturation[8 * h : 8 * h + 8] for h in range(2) for c in range(3)]
    y = product(jnp.concatenate(rows, 0), wyh[...], wyl[...])
    even, low = even_lanes(), low_lanes(8)
    for c in range(3):
        for p in range(8):
            upper = y[8 * c : 8 * c + 8, 128 * p : 128 * p + 128]
            lower = y[24 + 8 * c : 32 + 8 * c, 128 * p : 128 * p + 128]
            first = jnp.where(even, upper, pltpu.roll(lower, 1, 1))
            second = jnp.where(even, pltpu.roll(upper, 127, 1), lower)
            for z, tile in ((p % 4 * 4, first), (p % 4 * 4 + 1, second)):
                turned = half_turn(tile)
                row = (p // 4 * 16 + z) * 12 + c * 4
                s1[pl.ds(row, 4), :] = jnp.where(low, tile, turned)[:4]
                s1[pl.ds(row + 24, 4), :] = jnp.where(low, turned, tile)[4:]


def turn_in(k, r1, s2):
    for c in range(3):
        x = jnp.concatenate([r1[pl.ds(k * 192 + c * 4 + r, 16, stride=12), :] for r in range(4)], 0)
        block = jnp.concatenate([x, pltpu.roll(x, 64, 1)], 0).T
        for b in range(2):
            s2[pl.ds(k * 192 + 2 * c + b, 32, stride=6), :] = block[32 * b : 32 * b + 32]


def spectral_tables(fy, tb):
    sub = lax.broadcasted_iota(jnp.int32, (8, 128), 0)
    fx = sub % 4 * 128 + lax.broadcasted_iota(jnp.int32, (8, 128), 1)
    second = sub // 4 == 1
    sign = jnp.where(second, 1.0, -1.0)
    edge_x = fx == 0
    edge_y = jnp.full((8, 128), fy) == 0
    for v in range(2):
        sine_y = second if v == 0 else jnp.logical_not(second)
        high_x = jnp.logical_and(edge_x, second)
        high_y = jnp.logical_and(edge_y, sine_y)
        wave_x = jnp.where(high_x, CELLS, fx).astype(f32) * (math.pi / side_length)
        wave_y = jnp.where(high_y, CELLS, fy).astype(f32) * (math.pi / side_length)
        k = jnp.sqrt(wave_x * wave_x + wave_y * wave_y)
        nonzero = k > 0.0
        safe = jnp.where(nonzero, k, 1.0)
        inverse = 1.0 / safe
        half = 0.5 * safe
        ratio = polynomial(half * half, SINH)
        self_part = jnp.where(nonzero, jnp.exp(-half) * ratio, 1.0)
        mutual = jnp.where(nonzero, half * ratio * ratio, 0.0)
        weight = jnp.where(edge_x, 1.0, 2.0) * jnp.where(edge_y, 1.0, 2.0) * (1.0 / (PAD * PAD))
        ux, uy = wave_x * inverse, wave_y * inverse
        tb[v, 0] = jnp.exp(-spacing * k)
        tb[v, 1] = weight * (1.0 - self_part)
        tb[v, 2] = weight * mutual
        tb[v, 3] = weight * self_part
        tb[v, 4] = jnp.where(edge_x, 0.0, sign * ux)
        tb[v, 5] = jnp.where(edge_y, 0.0, sign * uy)
        tb[v, 6] = jnp.where(high_x, ux, 0.0)
        tb[v, 7] = jnp.where(high_y, uy, 0.0)


ORDER = [(0, 0), (1, 1), (0, 1), (1, 0)]
ORDER_X = [(1, 1), (0, 0), (1, 0), (0, 1)]


def tile_row(c, tg, cls, lb):
    return ((c * 2 + tg) * 16 + cls * 4 + lb) * 8


def transform_x(r2, wxh, wxl, zs):
    columns = []
    for x_lo in range(2):
        for h in range(2):
            parts = [r2[pl.ds(x_lo * 12 + h * 6 + q, 16, stride=24), :] for q in range(6)]
            columns.append(jnp.concatenate(parts, 0))
    z = product(jnp.concatenate(columns, 1), wxh[...], wxl[...])
    for c in range(3):
        for cls, (a, b) in enumerate(ORDER_X if c == 0 else ORDER):
            for tg in range(2):
                for lb in range(4):
                    row = (2 * c + b) * 16 + tg * 8
                    lane = a * 512 + lb * 128
                    zs[pl.ds(tile_row(c, tg, cls, lb), 8), :] = z[row : row + 8, lane : lane + 128]


def couple(zs, tb, ws):
    def at(c, t, v):
        return pl.ds(tile_row(c, t // 8, 2 * v, 0) + t % 8, 8, stride=8)

    for v in range(2):
        other = 1 - v
        decay, direct, mutual = tb[v, 0], tb[v, 1], tb[v, 2]
        ux, uy, lone_x, lone_y = tb[v, 4], tb[v, 5], tb[v, 6], tb[v, 7]
        if v == 1:
            uy = -uy
        carry = jnp.zeros((8, 128), f32)
        carry_lone = jnp.zeros((8, 128), f32)
        for t in range(LAYERS):
            r = ux * zs[at(0, t, other), :] + uy * zs[at(1, t, other), :]
            lone = lone_x * pltpu.roll(zs[at(0, t, v), :], 4, 0) + lone_y * zs[at(1, t, v), :]
            ws[v, t, 0] = r
            ws[v, t, 1] = lone
            ws[v, t, 2] = carry
            ws[v, t, 3] = carry_lone
            carry = decay * (carry + (zs[at(2, t, v), :] + r))
            carry_lone = decay * (carry_lone + lone)
    for v in range(2):
        decay, direct, mutual = tb[v, 0], tb[v, 1], tb[v, 2]
        carry = jnp.zeros((8, 128), f32)
        carry_lone = jnp.zeros((8, 128), f32)
        for t in range(LAYERS - 1, -1, -1):
            r, lone = ws[v, t, 0], ws[v, t, 1]
            below, below_lone = ws[v, t, 2], ws[v, t, 3]
            z = zs[at(2, t, v), :]
            ws[v, t, 0] = direct * r + mutual * (below + carry)
            ws[v, t, 1] = direct * lone + mutual * (below_lone + carry_lone)
            zs[at(2, t, v), :] = mutual * (below - carry) - tb[v, 3] * z
            carry = decay * (carry + (r - z))
            carry_lone = decay * (carry_lone + lone)
    for v in range(2):
        other = 1 - v
        ux, uy, lone_x, lone_y = tb[other, 4], tb[v, 5], tb[v, 6], tb[v, 7]
        if v == 1:
            uy = -uy
        for t in range(LAYERS):
            h, lone = ws[other, t, 0], ws[v, t, 1]
            zs[at(0, t, v), :] = -ux * h - pltpu.roll(lone_x * lone, 4, 0)
            zs[at(1, t, v), :] = uy * h - lone_y * lone


def return_x(zs, xwh, xwl, s3):
    rows = []
    for c in range(3):
        order = ORDER_X if c == 0 else ORDER
        for b in range(2):
            for tg in range(2):
                lanes = [
                    zs[pl.ds(tile_row(c, tg, order.index((a, b)), lb), 8), :] for a in range(2) for lb in range(4)
                ]
                rows.append(jnp.concatenate(lanes, 1))
    out = product(jnp.concatenate(rows, 0), xwh[...], xwl[...])
    for x_lo in range(2):
        for h in range(2):
            lane = (x_lo * 2 + h) * 128
            for q in range(6):
                s3[pl.ds(x_lo * 12 + h * 6 + q, 16, stride=24), :] = out[16 * q : 16 * q + 16, lane : lane + 128]


def turn_out(k, r3, s4):
    low = low_lanes(64)
    for c in range(3):
        parts = [r3[pl.ds(k * 192 + 2 * c + b, 32, stride=6), :] for b in range(2)]
        block = jnp.concatenate(parts + parts, 0).T
        block = jnp.where(low, block[:64], block[64:])
        for r in range(4):
            s4[pl.ds(k * 192 + c * 4 + r, 16, stride=12), :] = block[16 * r : 16 * r + 16]


def inverse_y(k, r4, ywh, ywl):
    even = even_lanes()
    kept = low_lanes(8) == (lax.broadcasted_iota(jnp.int32, (8, 128), 0) < 4)

    def tile(z, c):
        row = k * 192 + z * 12 + c * 4
        both = jnp.concatenate([r4[pl.ds(row, 4), :], r4[pl.ds(row + 24, 4), :]], 0)
        return jnp.where(kept, both, half_turn(both))

    upper, lower = [], []
    for c in range(3):
        up, low = [], []
        for p in range(4):
            first, second = tile(4 * p, c), tile(4 * p + 1, c)
            up.append(jnp.where(even, first, pltpu.roll(second, 1, 1)))
            low.append(jnp.where(even, pltpu.roll(first, 127, 1), second))
        upper.append(jnp.concatenate(up, 1))
        lower.append(jnp.concatenate(low, 1))
    wanted = slice(512 * k, 512 * k + 512)
    return product(jnp.concatenate(upper + lower, 0), ywh[wanted], ywl[wanted])


def cross_product(a, b):
    return (a[1] * b[2] - a[2] * b[1], a[2] * b[0] - a[0] * b[2], a[0] * b[1] - a[1] * b[0])


def other_fields(m, first_row, last_row, lower_m, upper_m, stiffness, lower_link, upper_link, anisotropy):
    lane = lax.broadcasted_iota(jnp.int32, (16, 512), 1)
    fields = []
    for c in range(3):
        beside = jnp.concatenate([first_row[c], m[c][:15]], 0) + jnp.concatenate([m[c][1:], last_row[c]], 0)
        beside = beside + jnp.where(lane == 0, 0.0, pltpu.roll(m[c], 1, 1))
        beside = beside + jnp.where(lane == 511, 0.0, pltpu.roll(m[c], 511, 1))
        fields.append(stiffness * beside + lower_link * lower_m[c] + upper_link * upper_m[c])
    fields[2] = fields[2] + anisotropy * m[2]
    return fields


def step(m, field):
    first = cross_product(m, field)
    second = cross_product(m, first)
    scale = -time_step / (1.0 + damping * damping)
    stepped = [m[c] + scale * (first[c] + damping * second[c]) for c in range(3)]
    inverse = lax.rsqrt(stepped[0] * stepped[0] + stepped[1] * stepped[1] + stepped[2] * stepped[2])
    return [s * inverse for s in stepped]


def kernel(
    polar_any, azimuth_any, saturation_any, anisotropy_any, stiffness_any, coupling_any,
    wyh_any, wyl_any, wxh_any, wxl_any, xwh_any, xwl_any, ywh_any, ywl_any,
    field_out, moment_out,
    polar, azimuth, saturation, anisotropy, stiffness, coupling,
    wyh, wyl, wxh, wxl, xwh, xwl, ywh, ywl, s1, r1, s2, r2, s3, r3, s4, r4, zs, ws, tb, near, edge_out, edge_in, rest,
    load_sem, send_sem, recv_sem, near_send, near_recv, edge_send, edge_recv,
):
    t = lax.axis_index("layer")
    p = lax.axis_index("plane")
    z = lax.rem(p, RING)
    x_lo = lax.div(p, RING)
    core = lax.rem(t, 2)
    y = lax.rem(lax.div(t, 2), 4)
    x_hi = lax.div(t, 8)
    source = t * 2 + x_lo
    owner = core * 16 + lax.div(t, 2) * 2 + x_lo

    def ring_device(away):
        there = lax.rem(z + away, RING)
        return there, (t, x_lo * RING + there)

    def slab_device(far, there_core):
        a, b, dy = far
        there_x = lax.rem(x_lo + b, 2)
        pair = lax.rem(x_hi + a, 2) * 4 + lax.rem(y + dy, 4)
        there_t = pair * 2 + there_core
        return there_t * 2 + there_x, there_core * 16 + pair * 2 + there_x, (there_t, there_x * RING + z)

    next_plane = (t, lax.rem(p + 1, 2 * RING))
    last_plane = (t, lax.rem(p + 2 * RING - 1, 2 * RING))
    next_layer = (lax.rem(t + 1, LAYERS), p)
    last_layer = (lax.rem(t + LAYERS - 1, LAYERS), p)

    barrier = pltpu.get_barrier_semaphore()

    def greet(there):
        pl.semaphore_signal(barrier, inc=1, device_id=there, device_id_type=MESH)

    for away in AWAY:
        greet(ring_device(away)[1])
    for far in FAR:
        greet(slab_device(far, 1 - core)[2])
        if any(far):
            greet(slab_device(far, core)[2])
    for there in (next_plane, last_plane):
        greet(there)

    loads = [
        pltpu.make_async_copy(src, dst, load_sem.at[i])
        for i, (src, dst) in enumerate([
            (polar_any, polar), (azimuth_any, azimuth), (saturation_any, saturation), (wyh_any, wyh), (wyl_any, wyl),
            (anisotropy_any, anisotropy), (stiffness_any, stiffness), (coupling_any, coupling),
            (wxh_any, wxh), (wxl_any, wxl), (xwh_any, xwh), (xwl_any, xwl), (ywh_any, ywh), (ywl_any, ywl),
        ])
    ]
    for load in loads:
        load.start()

    loads[0].wait()
    loads[1].wait()
    m = unit_moment(polar[0], azimuth[0])
    edge_out[...] = jnp.zeros((2, 16, 128), f32)
    for side, row in enumerate((0, 15)):
        for c in range(3):
            for lb in range(4):
                edge_out[side, c * 4 + lb : c * 4 + lb + 1, :] = m[c][row : row + 1, 128 * lb : 128 * lb + 128]
    for load in loads[2:5]:
        load.wait()
    forward_y(m, saturation[0], wyh, wyl, s1)

    pl.semaphore_wait(barrier, RING - 1 + SLAB - 1 + 2)

    def remote(src, dst, sem, there):
        return pltpu.make_async_remote_copy(
            src_ref=src, dst_ref=dst, send_sem=sem[0], recv_sem=sem[1], device_id=there, device_id_type=MESH
        )

    def rows_of(ref, i):
        return ref.at[pl.ds(pl.multiple_of(i * 12, 4), 12)]

    def ring_send(src, dst, n, k, arrival):
        for away in AWAY:
            there, device = ring_device(away)
            sems = (send_sem.at[n], recv_sem.at[arrival])
            remote(rows_of(src, k * 16 + there), rows_of(dst, k * 16 + z), sems, device).start()
        pltpu.make_async_copy(rows_of(src, k * 16 + z), rows_of(dst, k * 16 + z), recv_sem.at[arrival]).start()

    def slab_send(k):
        sems = (send_sem.at[1], recv_sem.at[2])
        for far in FAR:
            _, there, device = slab_device(far, k)
            if any(far):
                remote(rows_of(s2, there), rows_of(r2, source), sems, device).start()
            else:

                @pl.when(core == k)
                def _():
                    pltpu.make_async_copy(rows_of(s2, owner), rows_of(r2, source), recv_sem.at[2]).start()

                @pl.when(core != k)
                def _():
                    remote(rows_of(s2, there), rows_of(r2, source), sems, device).start()

    def slab_return():
        sems = (send_sem.at[2], recv_sem.at[3 + core])
        for far in FAR:
            for there_core in (1 - core, core):
                there, _, device = slab_device(far, there_core)
                if any(far) or there_core is not core:
                    remote(rows_of(s3, there), rows_of(r3, owner), sems, device).start()
        pltpu.make_async_copy(rows_of(s3, source), rows_of(r3, owner), recv_sem.at[3 + core]).start()

    def received(dst, n, rows=192):
        part = dst.at[pl.ds(0, rows)]
        pltpu.make_async_copy(part, part, recv_sem.at[n]).wait()

    for k in range(2):
        ring_send(s1, r1, 0, k, k)
    sides = []
    for i, (ref, side, there) in enumerate(
        [(polar, 0, next_layer), (azimuth, 0, next_layer), (polar, 1, last_layer), (azimuth, 1, last_layer)]
    ):
        sides.append(remote(ref.at[0], near.at[side, i % 2], (near_send.at[i], near_recv.at[i]), there))
    for side, there in ((0, last_plane), (1, next_plane)):
        sides.append(
            remote(edge_out.at[side], edge_in.at[1 - side], (edge_send.at[side], edge_recv.at[side]), there)
        )
    for copy in sides:
        copy.start()

    for load in loads[5:]:
        load.wait()
    spectral_tables(z * SLAB + owner, tb)
    for k in range(2):
        received(r1, k)
        turn_in(k, r1, s2)
        slab_send(k)
    for copy in sides:
        copy.wait_recv()
    lower_m = unit_moment(near[0, 0], near[0, 1])
    upper_m = unit_moment(near[1, 0], near[1, 1])
    lower_link = jnp.where(t > 0, coupling[jnp.maximum(t - 1, 0)], 0.0)
    upper_link = jnp.where(t < LAYERS - 1, coupling[jnp.minimum(t, LAYERS - 2)], 0.0)

    def edge_row(side, present):
        rows = []
        for c in range(3):
            lanes = [edge_in[side, c * 4 + lb : c * 4 + lb + 1, :] for lb in range(4)]
            rows.append(jnp.where(present, jnp.concatenate(lanes, 1), 0.0))
        return rows

    m = unit_moment(polar[0], azimuth[0])
    fields = other_fields(
        m, edge_row(0, p > 0), edge_row(1, p < 2 * RING - 1), lower_m, upper_m,
        stiffness[0], lower_link, upper_link, anisotropy[0],
    )
    for c in range(3):
        rest[c] = fields[c]
        rest[3 + c] = m[c]

    received(r2, 2, 384)
    transform_x(r2, wxh, wxl, zs)
    couple(zs, tb, ws)
    return_x(zs, xwh, xwl, s3)
    slab_return()
    for k in range(2):
        received(r3, 3 + k)
        turn_out(k, r3, s4)
        ring_send(s4, r4, 3, k, 5 + k)
    received(r4, 5)
    demag = inverse_y(0, r4, ywh, ywl)
    received(r4, 6)
    demag = demag + inverse_y(1, r4, ywh, ywl)
    m = [rest[3 + c] for c in range(3)]
    field = [
        jnp.concatenate([demag[8 * c : 8 * c + 8], demag[24 + 8 * c : 32 + 8 * c]], 0) + rest[c] for c in range(3)
    ]
    moment = step(m, field)
    for c in range(3):
        field_out[0, c] = field[c]
        moment_out[0, c] = moment[c]

    for copy in sides:
        copy.wait_send()
    for n, rows in ((0, 360), (1, 372), (2, 372), (3, 360)):
        part = s1.at[pl.ds(0, rows)]
        pltpu.make_async_copy(part, part, send_sem.at[n]).wait()


def body(polar, azimuth, saturation, anisotropy, stiffness, coupling):
    vmem = pl.BlockSpec(memory_space=pltpu.VMEM)
    hbm = pl.BlockSpec(memory_space=pltpu.HBM)
    out = pltpu.VMEM((1, 3, 16, CELLS), f32)
    dma = pltpu.SemaphoreType.DMA
    table, turned = pltpu.VMEM((CELLS, PAD), bf16), pltpu.VMEM((PAD, CELLS), bf16)
    block = pltpu.VMEM((SLAB * 12, 128), f32)
    row_block = pltpu.VMEM((1, 16, CELLS), f32)
    return pl.pallas_call(
        kernel,
        out_shape=(out, out),
        in_specs=[hbm] * 14,
        out_specs=(vmem, vmem),
        scratch_shapes=[
            row_block, row_block, row_block, row_block,
            pltpu.SMEM((1,), f32), pltpu.SMEM((LAYERS - 1,), f32),
            table, table, table, table, turned, turned, turned, turned,
            block, block, block, block, block, block, block, block,
            pltpu.VMEM((3 * 2 * 16 * 8, 128), f32),
            pltpu.VMEM((2, LAYERS, 4, 8, 128), f32),
            pltpu.VMEM((2, 8, 8, 128), f32),
            pltpu.VMEM((2, 2, 16, CELLS), f32),
            pltpu.VMEM((2, 16, 128), f32),
            pltpu.VMEM((2, 16, 128), f32),
            pltpu.VMEM((6, 16, CELLS), f32),
            dma((14,)), dma((4,)), dma((7,)), dma((4,)), dma((4,)), dma((2,)), dma((2,)),
        ],
        compiler_params=pltpu.CompilerParams(
            collective_id=0, has_side_effects=True, vmem_limit_bytes=60 * 1024 * 1024
        ),
        cost_estimate=pl.CostEstimate(flops=10**9, bytes_accessed=5 * 10**6, transcendentals=0),
        name="fields",
    )(polar, azimuth, saturation, anisotropy, stiffness, coupling, *transforms())


def solution(mesh):
    placed = (
        P("layer", "plane", None),
        P("layer", "plane", None),
        P("layer", "plane", None),
        P("layer", "plane", None),
        P("layer"),
        P(),
    )
    return jax.shard_map(
        body,
        mesh=mesh,
        in_specs=placed,
        out_specs=(P("layer", None, "plane", None), P("layer", None, "plane", None)),
        check_vma=False,
    )
```
